512 devices in a mesh: seq: 128 (over y, z, core), blk: 4 (over x).
Axes of the slice: x: 4, y: 8, z: 8, core: 2. Of those that a mesh axis runs over, the one named last changes fastest.
Arguments:
- queries: bfloat16 [65536, 4096], P(('seq', 'blk')), may hold values from -24 to 24
- keys: bfloat16 [65536, 4096], P(('seq', 'blk')), may hold values from -24 to 24
- values: bfloat16 [65536, 4096], P(('seq', 'blk')), may hold values from -6 to 6
- cluster_ids: int32 [65536, 1], P(('seq', 'blk')), may hold values from 0 to 127; in each aligned block of 128 rows (0 to 127, 128 to 255, ...) at most 2 rows name the same one
Outputs:
- attended: bfloat16 [65536, 4096], P(('seq', 'blk'))
The draws below stay inside these ranges and needn't reach their ends.
Inputs may be any that keep to these rules, and one draw needn't show every extreme that they name: `cluster_ids`: at most 2 tokens of one device share a cluster, and that many are reached.
All inputs are finite; a program needn't handle non-finite values.
Results may differ from the reference program's by a relative error of at most 0.0085.
Values may be sent and summed in bfloat16 or wider, within the bound.
No kernel may reach another device: no remote copies, remote signals or barrier semaphores. Data moves between devices by JAX's collectives and lax.ppermute only.
A program may use at most 64 MiB of HBM per device.

```python
import math
import jax
import jax.numpy as jnp
import numpy as np
from jax import lax

HEADS = 32
HEAD = 128
TOK_DEV = 128
TOKENS = 65536
NCLUST = 128
MOST = 2
CAP = 1024


def draw_queries(key, part):
    key = jax.random.fold_in(key, 11)
    field = jnp.clip(jax.random.normal(key, (TOKENS, HEADS, HEAD), jnp.float32), -6.0, 6.0)
    return field.reshape(TOKENS, HEADS * HEAD).astype(jnp.bfloat16)


def draw_keys(key, part):
    key = jax.random.fold_in(key, 23)
    field = jnp.clip(jax.random.normal(key, (TOKENS, HEADS, HEAD), jnp.float32), -6.0, 6.0)
    return field.reshape(TOKENS, HEADS * HEAD).astype(jnp.bfloat16)


def block_scale(key, extent, shards, least, high):
    def one(position, parts):
        heights = jax.random.uniform(jax.random.fold_in(jax.random.fold_in(key, 6), position), (parts,), jnp.float32, least / len(shards), high / len(shards))
        return jnp.repeat(jnp.exp(heights), extent[position] // parts).reshape((-1,) + (1,) * (len(extent) - position - 1))

    level = one(*shards[0])
    for cut in shards[1:]:
        level = level * one(*cut)
    return level


def routed_block(rng, own, number, rows, count, top, limit, skew):
    sequence = jax.random.permutation(rng, count)
    crowded, common = portions_of(count, rows * top, limit, skew, True), portions_of(count, rows * top, limit, skew, False)
    places = jnp.arange(count)

    def named(lengths, rotation):
        used = int((lengths > 0).sum())
        fixed = max(1, used // 4)
        passed = fixed + (places - fixed + rotation * (used - fixed)) % max(1, count - fixed)
        return jnp.zeros((count,), jnp.int32).at[sequence[jnp.where(places < fixed, places, passed)]].set(jnp.asarray(lengths, jnp.int32))

    lengths = jnp.where(number % 4 == 0, named(crowded, number // 4), named(common, number - number // 4 - 1))
    mixed = jax.random.permutation(jax.random.fold_in(own, 3), count)
    giver, taker = mixed[0:count // 2 * 2:2], mixed[1:count // 2 * 2:2]
    margin = jnp.minimum(lengths[giver] - 1, limit - lengths[taker]) // 2
    margin = jnp.where((giver == sequence[0]) | (taker == sequence[0]) | (lengths[taker] == 0), 0, jnp.maximum(margin, 0))
    passed = jax.random.randint(jax.random.fold_in(own, 4), (count // 2,), 0, 1 << 20) % (margin + 1)
    lengths = lengths.at[giver].add(-passed).at[taker].add(passed)
    items = jnp.searchsorted(jnp.cumsum(lengths), jnp.arange(rows * top), side="right").astype(jnp.int32)
    grid = items.reshape(top, rows).T
    grid = grid[jax.random.permutation(jax.random.fold_in(own, 1), rows)]
    rotation = jax.random.randint(jax.random.fold_in(own, 2), (rows, 1), 0, top)
    return jnp.take_along_axis(grid, (jnp.arange(top)[None, :] + rotation) % top, axis=1)


def portions_of(number_of, total, limit, slope, full):
    weights = [(1 << 20) // math.isqrt(grade ** slope) + 1 for grade in range(1, number_of + 1)]
    largest = limit if full else min(limit, max(-(-total // number_of), total * weights[0] // sum(weights)))
    least = 1 if total - largest >= number_of - 1 else 0
    counts, spare = [largest] + [least] * (number_of - 1), total - largest - least * (number_of - 1)
    while spare > 0:
        candidates = [i for i in range(1, number_of) if counts[i] < largest] or [i for i in range(1, number_of) if counts[i] < limit]
        pool, budget = sum([weights[i] for i in candidates]), spare
        for i in candidates:
            extra = min(limit - counts[i], max(1, budget * weights[i] // pool), spare)
            counts[i] = counts[i] + extra
            spare = spare - extra
    return np.array(counts)


def gaussian(key, dims, deviation, reach, pieces=(), kind=jnp.bfloat16):
    entries = jax.random.normal(key, dims, jnp.float32) * deviation
    if len(pieces) > 0:
        entries = block_scale(key, dims, pieces, -0.22, 0.18) * entries
    return jnp.clip(entries, min=-reach, max=reach).astype(kind)


def setup_inputs(seed: int = 0) -> dict:
    seeds = jax.random.split(jax.random.key(seed), 5)
    queries = draw_queries(jax.random.fold_in(seeds[4], 71), 0)
    keys = draw_keys(jax.random.fold_in(seeds[4], 71), 0)
    values = gaussian(seeds[2], (TOKENS, HEADS * HEAD), 1.0, 6.0, ((0, 512),))
    cluster_ids_keys = jax.random.split(jax.random.fold_in(seeds[3], 1), TOKENS // TOK_DEV)
    cluster_ids_turns = jax.random.permutation(jax.random.fold_in(seeds[3], 3), TOKENS // TOK_DEV)
    cluster_ids = jax.vmap(lambda own, number: routed_block(jax.random.fold_in(seeds[3], 2), own, number, TOK_DEV, NCLUST, 1, MOST, 2))(cluster_ids_keys, cluster_ids_turns).reshape((TOKENS, 1))
    return dict(queries=queries, keys=keys, values=values, cluster_ids=cluster_ids)


def reference(queries, keys, values, cluster_ids):
    cluster = cluster_ids[:, 0].astype(jnp.int32)
    order = jnp.argsort(cluster, stable=True).astype(jnp.int32)
    sorted_cluster = cluster[order]
    q_rows = queries[order].reshape(TOKENS, HEADS, HEAD)
    k_rows = keys[order].reshape(TOKENS, HEADS, HEAD)
    v_rows = values[order].reshape(TOKENS, HEADS, HEAD)
    k_padded = jnp.concatenate([jnp.zeros((CAP, HEADS, HEAD), k_rows.dtype), k_rows], axis=0)
    v_padded = jnp.concatenate([jnp.zeros((CAP, HEADS, HEAD), v_rows.dtype), v_rows], axis=0)
    c_padded = jnp.concatenate([jnp.full((CAP,), -1, dtype=jnp.int32), sorted_cluster], axis=0)
    p_padded = jnp.concatenate([jnp.full((CAP,), -1, dtype=jnp.int32), order], axis=0)
    block = min(512, TOKENS)
    scale = 1.0 / (HEAD ** 0.5)

    def one_block(index):
        start = index * block
        q_block = lax.dynamic_slice_in_dim(q_rows, start, block, 0).astype(jnp.float32)
        c_query = lax.dynamic_slice_in_dim(sorted_cluster, start, block, 0)
        p_query = lax.dynamic_slice_in_dim(order, start, block, 0)
        k_block = lax.dynamic_slice_in_dim(k_padded, start, CAP + block, 0).astype(jnp.float32)
        v_block = lax.dynamic_slice_in_dim(v_padded, start, CAP + block, 0).astype(jnp.float32)
        c_key = lax.dynamic_slice_in_dim(c_padded, start, CAP + block, 0)
        p_key = lax.dynamic_slice_in_dim(p_padded, start, CAP + block, 0)
        scores = jnp.einsum("qhd,khd->hqk", q_block, k_block) * scale
        allowed = (c_key[None, :] == c_query[:, None]) & (p_key[None, :] <= p_query[:, None])
        scores = jnp.where(allowed[None], scores, -1e30)
        top = jnp.max(scores, axis=-1, keepdims=True)
        weights = jnp.where(allowed[None], jnp.exp(scores - top), 0.0)
        total = jnp.sum(weights, axis=-1, keepdims=True)
        rounded = weights.astype(jnp.bfloat16).astype(jnp.float32)
        mixed = jnp.einsum("hqk,khd->hqd", rounded, v_block) / total
        return jnp.transpose(mixed, (1, 0, 2)).astype(jnp.bfloat16)

    outs = lax.map(one_block, jnp.arange(TOKENS // block, dtype=jnp.int32))
    outs = outs.reshape(TOKENS, HEADS * HEAD)
    return jnp.zeros_like(queries).at[order].set(outs)
```

```python
import jax
import jax.numpy as jnp
from jax import lax
from jax.experimental import pallas as pl
from jax.experimental.pallas import tpu as pltpu
from jax.sharding import PartitionSpec as P

HEADS = 32
HEAD = 128
TOK = 128
CLUSTERS = 128
MOST = 2
GROUPS = 4
SHARE = HEADS // GROUPS
UNIT = SHARE * MOST
DEVICES = CLUSTERS * GROUPS
ROWS = DEVICES * MOST
QBLK = 256
EMPTY = 256.0
MASKED = -1e30
FACTOR = 1.4426950408889634 / HEAD**0.5
BF16 = jnp.bfloat16
F32 = jnp.float32


def iota(shape, dim):
    return lax.broadcasted_iota(jnp.int32, shape, dim)


def swap_matrix():
    size = SHARE * UNIT
    out, src = iota((size, size), 0), iota((size, size), 1)
    a, b, s = out // UNIT, (out // MOST) % SHARE, out % MOST
    return (src == b * UNIT + a * MOST + s).astype(F32).astype(BF16)


def slot_row(col, row):
    same = (col == row) & (iota((TOK, TOK), 0) < iota((TOK, TOK), 1))
    within = jnp.sum(same.astype(F32), axis=0, keepdims=True)
    return row.astype(F32) * MOST + within


def dot(a, b):
    return jnp.dot(a, b, preferred_element_type=F32)


def pack_kernel(col_ref, row_ref, q_ref, k_ref, v_ref, out_ref):
    slots = slot_row(col_ref[...], row_ref[...])
    numbers = iota((CLUSTERS * MOST, TOK), 0).astype(F32)
    onehot = (numbers == slots).astype(F32)
    filled = jnp.sum(onehot, axis=1, keepdims=True) > 0.5
    onehot = onehot.astype(BF16)
    first_lane = (iota((CLUSTERS * MOST, SHARE * HEAD), 1) % HEAD) == 0
    swap = swap_matrix()
    for index, ref in enumerate((q_ref, k_ref, v_ref)):
        rows = dot(onehot, ref[...])
        if index == 1:
            rows = jnp.where(first_lane & jnp.logical_not(filled), EMPTY, rows)
        rows = rows.astype(BF16)
        for block in range(CLUSTERS // SHARE):
            part = rows[block * UNIT : (block + 1) * UNIT, :]
            tall = jnp.concatenate(
                [part[:, h * HEAD : (h + 1) * HEAD] for h in range(SHARE)], axis=0
            )
            mixed = dot(swap, tall).astype(BF16)
            out_ref[
                block * SHARE : (block + 1) * SHARE, 0, index * UNIT : (index + 1) * UNIT, :
            ] = mixed.reshape(SHARE, UNIT, HEAD)


def pack(col, row, queries, keys, values):
    data = pl.BlockSpec((TOK, SHARE * HEAD), lambda g: (0, g))
    return pl.pallas_call(
        pack_kernel,
        grid=(GROUPS,),
        in_specs=[
            pl.BlockSpec((TOK, 1), lambda g: (0, 0)),
            pl.BlockSpec((1, TOK), lambda g: (0, 0)),
            data,
            data,
            data,
        ],
        out_specs=pl.BlockSpec((CLUSTERS, 1, 3 * UNIT, HEAD), lambda g: (0, g, 0, 0)),
        out_shape=jax.ShapeDtypeStruct((CLUSTERS, GROUPS, 3 * UNIT, HEAD), BF16),
        compiler_params=pltpu.CompilerParams(vmem_limit_bytes=32 * 1024 * 1024),
        name="pack",
    )(col, row, queries, keys, values)


def attend_kernel(in_ref, out_ref, q_scr, k_scr, v_scr, o_scr, bias_scr):
    swap = swap_matrix()

    def regroup(block, carry):
        first = pl.multiple_of(block * SHARE, SHARE)
        start = pl.multiple_of(block * UNIT, UNIT)
        part = in_ref[pl.ds(first, SHARE), :, :]
        for index, ref in enumerate((q_scr, k_scr, v_scr)):
            tall = part[:, index * UNIT : (index + 1) * UNIT, :].reshape(SHARE * UNIT, HEAD)
            mixed = dot(swap, tall).astype(BF16)
            ref[:, pl.ds(start, UNIT), :] = mixed.reshape(SHARE, UNIT, HEAD)
        return carry

    lax.fori_loop(0, DEVICES // SHARE, regroup, 0, unroll=4)

    pick = (iota((8, HEAD), 1) == 0).astype(F32).astype(BF16)
    marks = lax.dot_general(
        pick, k_scr[0], (((1,), (1,)), ((), ())), preferred_element_type=F32
    )
    bias_scr[...] = jnp.where(marks > EMPTY / 2, MASKED, 0.0)

    def one_head(h, carry):
        for block in range(ROWS // QBLK):
            start, stop = block * QBLK, (block + 1) * QBLK
            q = q_scr[h, start:stop, :]
            k = k_scr[h, 0:stop, :]
            v = v_scr[h, 0:stop, :]
            scores = lax.dot_general(
                q, k, (((1,), (1,)), ((), ())), preferred_element_type=F32
            )
            scores = scores + bias_scr[0:1, 0:stop]
            later = iota((QBLK, QBLK), 1) > iota((QBLK, QBLK), 0)
            last = jnp.where(later, MASKED, scores[:, start:stop])
            if block:
                scores = jnp.concatenate([scores[:, :start], last], axis=1)
            else:
                scores = last
            top = jnp.max(scores, axis=1, keepdims=True)
            weights = jnp.exp2((scores - top) * FACTOR)
            total = jnp.sum(weights, axis=1, keepdims=True)
            mixed = dot(weights.astype(BF16), v) / total
            o_scr[h, start:stop, :] = mixed.astype(BF16)
        return carry

    lax.fori_loop(0, SHARE, one_head, 0)

    def ungroup(block, carry):
        first = pl.multiple_of(block * SHARE, SHARE)
        start = pl.multiple_of(block * UNIT, UNIT)
        tall = o_scr[:, pl.ds(start, UNIT), :].reshape(SHARE * UNIT, HEAD)
        mixed = dot(swap, tall).astype(BF16)
        out_ref[pl.ds(first, SHARE), :, :] = mixed.reshape(SHARE, UNIT, HEAD)
        return carry

    lax.fori_loop(0, DEVICES // SHARE, ungroup, 0, unroll=4)


def attend(received):
    held = pltpu.VMEM((SHARE, ROWS, HEAD), BF16)
    return pl.pallas_call(
        attend_kernel,
        in_specs=[pl.BlockSpec(memory_space=pltpu.VMEM)],
        out_specs=pl.BlockSpec(memory_space=pltpu.VMEM),
        out_shape=jax.ShapeDtypeStruct((DEVICES, UNIT, HEAD), BF16),
        scratch_shapes=[held, held, held, held, pltpu.VMEM((8, ROWS), F32)],
        compiler_params=pltpu.CompilerParams(vmem_limit_bytes=48 * 1024 * 1024),
        name="attend",
    )(received)


def unpack_kernel(col_ref, row_ref, in_ref, out_ref):
    slots = slot_row(col_ref[...], row_ref[...])
    numbers = iota((CLUSTERS * MOST, TOK), 0).astype(F32)
    onehot = (numbers == slots).astype(F32).astype(BF16)
    swap = swap_matrix()
    blocks = []
    for block in range(CLUSTERS // SHARE):
        tall = in_ref[block * SHARE : (block + 1) * SHARE, 0, :, :].reshape(SHARE * UNIT, HEAD)
        mixed = dot(swap, tall).astype(BF16)
        blocks.append(
            jnp.concatenate([mixed[h * UNIT : (h + 1) * UNIT, :] for h in range(SHARE)], axis=1)
        )
    rows = jnp.concatenate(blocks, axis=0)
    out_ref[...] = lax.dot_general(
        onehot, rows, (((0,), (0,)), ((), ())), preferred_element_type=F32
    ).astype(BF16)


def unpack(col, row, back):
    return pl.pallas_call(
        unpack_kernel,
        grid=(GROUPS,),
        in_specs=[
            pl.BlockSpec((TOK, 1), lambda g: (0, 0)),
            pl.BlockSpec((1, TOK), lambda g: (0, 0)),
            pl.BlockSpec((CLUSTERS, 1, UNIT, HEAD), lambda g: (0, g, 0, 0)),
        ],
        out_specs=pl.BlockSpec((TOK, SHARE * HEAD), lambda g: (0, g)),
        out_shape=jax.ShapeDtypeStruct((TOK, HEADS * HEAD), BF16),
        compiler_params=pltpu.CompilerParams(vmem_limit_bytes=32 * 1024 * 1024),
        name="unpack",
    )(col, row, back)


def exchange(data):
    return lax.all_to_all(data, ("seq", "blk"), split_axis=0, concat_axis=0, tiled=True)


def body(queries, keys, values, cluster_ids):
    row = cluster_ids.reshape(1, TOK)
    sent = pack(cluster_ids, row, queries, keys, values)
    received = exchange(sent.reshape(DEVICES, 3 * UNIT, HEAD))
    mixed = attend(received)
    back = exchange(mixed)
    return unpack(cluster_ids, row, back.reshape(CLUSTERS, GROUPS, UNIT, HEAD))


def solution(mesh):
    spec = P(("seq", "blk"), None)
    return jax.shard_map(
        body, mesh=mesh, in_specs=(spec,) * 4, out_specs=spec, check_vma=False
    )
```

```python
import jax
import jax.numpy as jnp
from jax import lax
from jax.experimental import pallas as pl
from jax.experimental.pallas import tpu as pltpu
from jax.sharding import PartitionSpec as P

HEADS = 32
HEAD = 128
TOK = 128
CLUSTERS = 128
MOST = 2
GROUPS = 4
SHARE = HEADS // GROUPS
UNIT = SHARE * MOST
DEVICES = CLUSTERS * GROUPS
ROWS = DEVICES * MOST
QBLK = 256
SOURCES = QBLK // MOST
CHUNK = 16
VMEM = 56 * 1024 * 1024
EMPTY = 256.0
MASKED = -1e30
FACTOR = 1.4426950408889634 / HEAD**0.5
BF16 = jnp.bfloat16
F32 = jnp.float32


def iota(shape, dim):
    return lax.broadcasted_iota(jnp.int32, shape, dim)


def spread_matrix(inverse):
    size = CHUNK * UNIT
    out, src = iota((size, size), 0), iota((size, size), 1)
    if inverse:
        out, src = src, out
    h, d, s = out // (CHUNK * MOST), (out // MOST) % CHUNK, out % MOST
    return (src == d * UNIT + h * MOST + s).astype(F32).astype(BF16)


def slot_onehot(row):
    row = row.astype(F32)
    above, across = iota((TOK, TOK), 0), iota((TOK, TOK), 1)
    col = jnp.sum(jnp.where(above == across, row, 0.0), axis=1, keepdims=True)
    earlier = (col == row) & (above < across)
    slots = row * MOST + jnp.sum(earlier.astype(F32), axis=0, keepdims=True)
    return (iota((CLUSTERS * MOST, TOK), 0).astype(F32) == slots).astype(F32)


def dot(a, b):
    return jnp.dot(a, b, preferred_element_type=F32)


def pack_kernel(row_ref, q_ref, k_ref, v_ref, out_ref):
    onehot = slot_onehot(row_ref[...])
    filled = jnp.sum(onehot, axis=1, keepdims=True) > 0.5
    onehot = onehot.astype(BF16)
    empty_entry = jnp.where(filled | (iota((1, HEAD), 1) > 0), 0.0, EMPTY)
    empty_entry = jnp.concatenate([empty_entry] * SHARE, axis=1)
    scatter = spread_matrix(True)
    rows = [dot(onehot, ref[...]) for ref in (q_ref, k_ref, v_ref)]
    rows[1] = rows[1] + empty_entry
    rows = [one.astype(BF16) for one in rows]
    width = CHUNK * MOST
    for block in range(CLUSTERS // CHUNK):
        tall = jnp.concatenate(
            [
                jnp.concatenate(
                    [
                        one[block * width : (block + 1) * width, h * HEAD : (h + 1) * HEAD]
                        for h in range(SHARE)
                    ],
                    axis=0,
                )
                for one in rows
            ],
            axis=1,
        )
        mixed = dot(scatter, tall).astype(BF16)
        for index in range(3):
            out_ref[
                block * CHUNK : (block + 1) * CHUNK, 0, index * UNIT : (index + 1) * UNIT, :
            ] = mixed[:, index * HEAD : (index + 1) * HEAD].reshape(CHUNK, UNIT, HEAD)


def pack(row, queries, keys, values):
    data = pl.BlockSpec((TOK, SHARE * HEAD), lambda g: (0, g))
    return pl.pallas_call(
        pack_kernel,
        grid=(GROUPS,),
        in_specs=[pl.BlockSpec((1, TOK), lambda g: (0, 0)), data, data, data],
        out_specs=pl.BlockSpec((CLUSTERS, 1, 3 * UNIT, HEAD), lambda g: (0, g, 0, 0)),
        out_shape=jax.ShapeDtypeStruct((CLUSTERS, GROUPS, 3 * UNIT, HEAD), BF16),
        compiler_params=pltpu.CompilerParams(vmem_limit_bytes=VMEM),
        name="pack",
    )(row, queries, keys, values)


def attend_kernel(in_ref, out_ref, k_scr, v_scr, q_scr, o_scr, mark_scr):
    step = pl.program_id(0)
    gather, scatter = spread_matrix(False), spread_matrix(True)
    first_lane = iota((QBLK, HEAD), 1) == 0

    def regroup(block):
        part = in_ref[block * CHUNK : (block + 1) * CHUNK, :, :]
        tall = jnp.concatenate(
            [
                part[:, i * UNIT : (i + 1) * UNIT, :].reshape(CHUNK * UNIT, HEAD)
                for i in range(3)
            ],
            axis=1,
        )
        mixed = dot(gather, tall).astype(BF16)
        width = CHUNK * MOST
        start = pl.multiple_of(step * QBLK + block * width, width)
        q_scr[:, block * width : (block + 1) * width, :] = mixed[:, :HEAD].reshape(
            SHARE, width, HEAD
        )
        k_scr[:, pl.ds(start, width), :] = mixed[:, HEAD : 2 * HEAD].reshape(SHARE, width, HEAD)
        v_scr[:, pl.ds(start, width), :] = mixed[:, 2 * HEAD :].reshape(SHARE, width, HEAD)

    for block in range(SOURCES // CHUNK):
        regroup(block)

    here = pl.multiple_of(step * QBLK, QBLK)
    empty = k_scr[0, pl.ds(here, QBLK), :].astype(F32) > EMPTY / 2
    mark_scr[pl.ds(here, QBLK), :] = jnp.where(empty & first_lane, MASKED, 0.0).astype(BF16)

    def queries_of(block):
        start, stop = block * QBLK, (block + 1) * QBLK
        unit = first_lane.astype(F32).astype(BF16)
        later = iota((QBLK, QBLK), 1) > iota((QBLK, QBLK), 0)
        ones = jnp.ones((stop, HEAD), BF16)
        for h in range(SHARE):
            q = jnp.concatenate([q_scr[h], unit], axis=1)
            k = jnp.concatenate([k_scr[h, 0:stop, :], mark_scr[0:stop, :]], axis=1)
            v = jnp.concatenate([v_scr[h, 0:stop, :], ones], axis=1)
            scores = lax.dot_general(
                q, k, (((1,), (1,)), ((), ())), preferred_element_type=F32
            )
            last = jnp.where(later, MASKED, scores[:, start:stop])
            if block:
                scores = jnp.concatenate([scores[:, :start], last], axis=1)
            else:
                scores = last
            top = jnp.max(scores, axis=1, keepdims=True)
            weights = jnp.exp2((scores - top) * FACTOR)
            mixed = dot(weights.astype(BF16), v)
            o_scr[h] = (mixed[:, :HEAD] / mixed[:, HEAD:]).astype(BF16)

    for block in range(ROWS // QBLK):
        pl.when(step == block)(lambda block=block: queries_of(block))

    for block in range(SOURCES // CHUNK):
        width = CHUNK * MOST
        tall = o_scr[:, block * width : (block + 1) * width, :].reshape(CHUNK * UNIT, HEAD)
        mixed = dot(scatter, tall).astype(BF16)
        out_ref[block * CHUNK : (block + 1) * CHUNK, :, :] = mixed.reshape(CHUNK, UNIT, HEAD)


def attend(received):
    held = pltpu.VMEM((SHARE, ROWS, HEAD), BF16)
    part = pltpu.VMEM((SHARE, QBLK, HEAD), BF16)
    return pl.pallas_call(
        attend_kernel,
        grid=(ROWS // QBLK,),
        in_specs=[pl.BlockSpec((SOURCES, 3 * UNIT, HEAD), lambda b: (b, 0, 0))],
        out_specs=pl.BlockSpec((SOURCES, UNIT, HEAD), lambda b: (b, 0, 0)),
        out_shape=jax.ShapeDtypeStruct((DEVICES, UNIT, HEAD), BF16),
        scratch_shapes=[held, held, part, part, pltpu.VMEM((ROWS, HEAD), BF16)],
        compiler_params=pltpu.CompilerParams(vmem_limit_bytes=VMEM),
        name="attend",
    )(received)


def unpack_kernel(row_ref, in_ref, out_ref):
    onehot = slot_onehot(row_ref[...]).astype(BF16)
    gather = spread_matrix(False)
    width = CHUNK * MOST
    blocks = []
    for block in range(CLUSTERS // CHUNK):
        tall = in_ref[block * CHUNK : (block + 1) * CHUNK, 0, :, :].reshape(CHUNK * UNIT, HEAD)
        mixed = dot(gather, tall).astype(BF16)
        blocks.append(
            jnp.concatenate([mixed[h * width : (h + 1) * width, :] for h in range(SHARE)], axis=1)
        )
    rows = jnp.concatenate(blocks, axis=0)
    out_ref[...] = lax.dot_general(
        onehot, rows, (((0,), (0,)), ((), ())), preferred_element_type=F32
    ).astype(BF16)


def unpack(row, back):
    return pl.pallas_call(
        unpack_kernel,
        grid=(GROUPS,),
        in_specs=[
            pl.BlockSpec((1, TOK), lambda g: (0, 0)),
            pl.BlockSpec((CLUSTERS, 1, UNIT, HEAD), lambda g: (0, g, 0, 0)),
        ],
        out_specs=pl.BlockSpec((TOK, SHARE * HEAD), lambda g: (0, g)),
        out_shape=jax.ShapeDtypeStruct((TOK, HEADS * HEAD), BF16),
        compiler_params=pltpu.CompilerParams(vmem_limit_bytes=VMEM),
        name="unpack",
    )(row, back)


def exchange(data):
    return lax.all_to_all(data, ("seq", "blk"), split_axis=0, concat_axis=0, tiled=True)


def body(queries, keys, values, cluster_ids):
    row = cluster_ids.reshape(1, TOK)
    sent = pack(row, queries, keys, values)
    received = exchange(sent.reshape(DEVICES, 3 * UNIT, HEAD))
    mixed = attend(received)
    back = exchange(mixed)
    return unpack(row, back.reshape(CLUSTERS, GROUPS, UNIT, HEAD))


def solution(mesh):
    spec = P(("seq", "blk"), None)
    return jax.shard_map(
        body, mesh=mesh, in_specs=(spec,) * 4, out_specs=spec, check_vma=False
    )
```

```python
import jax
import jax.numpy as jnp
from jax import lax
from jax.experimental import pallas as pl
from jax.experimental.pallas import tpu as pltpu
from jax.sharding import PartitionSpec as P

HEADS = 32
HEAD = 128
TOK = 128
CLUSTERS = 128
MOST = 2
GROUPS = 4
SHARE = HEADS // GROUPS
UNIT = SHARE * MOST
DEVICES = CLUSTERS * GROUPS
ROWS = DEVICES * MOST
QBLK = 256
SOURCES = QBLK // MOST
CHUNK = 16
VMEM = 56 * 1024 * 1024
EXTRA = 5
TAIL = 16
MESSAGE = 3 * SHARE + TAIL
NONE = -64.0
EMPTY = 256.0
MASKED = -1e30
FACTOR = 1.4426950408889634 / HEAD**0.5
BF16 = jnp.bfloat16
F32 = jnp.float32


def iota(shape, dim):
    return lax.broadcasted_iota(jnp.int32, shape, dim)


def spread_matrix(inverse):
    size = CHUNK * UNIT
    out, src = iota((size, size), 0), iota((size, size), 1)
    if inverse:
        out, src = src, out
    h, d, s = out // (CHUNK * MOST), (out // MOST) % CHUNK, out % MOST
    return (src == d * UNIT + h * MOST + s).astype(F32).astype(BF16)


def slot_onehot(row):
    row = row.astype(F32)
    above, across = iota((TOK, TOK), 0), iota((TOK, TOK), 1)
    col = jnp.sum(jnp.where(above == across, row, 0.0), axis=1, keepdims=True)
    earlier = (col == row) & (above < across)
    slots = row * MOST + jnp.sum(earlier.astype(F32), axis=0, keepdims=True)
    return (iota((CLUSTERS * MOST, TOK), 0).astype(F32) == slots).astype(F32)


def dot(a, b):
    return jnp.dot(a, b, preferred_element_type=F32)


def pack_kernel(row_ref, q_ref, k_ref, v_ref, out_ref):
    onehot = slot_onehot(row_ref[...])
    filled = jnp.sum(onehot, axis=1, keepdims=True) > 0.5
    onehot = onehot.astype(BF16)
    empty_entry = jnp.where(filled | (iota((1, HEAD), 1) > 0), 0.0, EMPTY)
    empty_entry = jnp.concatenate([empty_entry] * SHARE, axis=1)
    scatter = spread_matrix(True)
    rows = [dot(onehot, ref[...]) for ref in (q_ref, k_ref, v_ref)]
    rows[1] = rows[1] + empty_entry
    rows = [one.astype(BF16) for one in rows]
    width = CHUNK * MOST
    for block in range(CLUSTERS // CHUNK):
        tall = jnp.concatenate(
            [
                jnp.concatenate(
                    [
                        one[block * width : (block + 1) * width, h * HEAD : (h + 1) * HEAD]
                        for h in range(SHARE)
                    ],
                    axis=0,
                )
                for one in rows
            ],
            axis=1,
        )
        mixed = dot(scatter, tall).astype(BF16)
        for index in range(3):
            out_ref[
                block * CHUNK : (block + 1) * CHUNK, 0, index * UNIT : (index + 1) * UNIT, :
            ] = mixed[:, index * HEAD : (index + 1) * HEAD].reshape(CHUNK, UNIT, HEAD)


def pack(row, queries, keys, values):
    data = pl.BlockSpec((TOK, SHARE * HEAD), lambda g: (0, g))
    return pl.pallas_call(
        pack_kernel,
        grid=(GROUPS,),
        in_specs=[pl.BlockSpec((1, TOK), lambda g: (0, 0)), data, data, data],
        out_specs=pl.BlockSpec((CLUSTERS, 1, 3 * UNIT, HEAD), lambda g: (0, g, 0, 0)),
        out_shape=jax.ShapeDtypeStruct((CLUSTERS, GROUPS, 3 * UNIT, HEAD), BF16),
        compiler_params=pltpu.CompilerParams(vmem_limit_bytes=VMEM),
        name="pack",
    )(row, queries, keys, values)


def attend_kernel(in_ref, out_ref, k_scr, v_scr, q_scr, o_scr, mark_scr):
    step = pl.program_id(0)
    gather, scatter = spread_matrix(False), spread_matrix(True)
    first_lane = iota((QBLK, HEAD), 1) == 0

    def regroup(block):
        part = in_ref[block * CHUNK : (block + 1) * CHUNK, :, :]
        tall = jnp.concatenate(
            [
                part[:, i * UNIT : (i + 1) * UNIT, :].reshape(CHUNK * UNIT, HEAD)
                for i in range(3)
            ],
            axis=1,
        )
        mixed = dot(gather, tall).astype(BF16)
        width = CHUNK * MOST
        start = pl.multiple_of(step * QBLK + block * width, width)
        q_scr[:, block * width : (block + 1) * width, :] = mixed[:, :HEAD].reshape(
            SHARE, width, HEAD
        )
        k_scr[:, pl.ds(start, width), :] = mixed[:, HEAD : 2 * HEAD].reshape(SHARE, width, HEAD)
        v_scr[:, pl.ds(start, width), :] = mixed[:, 2 * HEAD :].reshape(SHARE, width, HEAD)

    for block in range(SOURCES // CHUNK):
        regroup(block)

    here = pl.multiple_of(step * QBLK, QBLK)
    empty = k_scr[0, pl.ds(here, QBLK), :].astype(F32) > EMPTY / 2
    mark_scr[pl.ds(here, QBLK), :] = jnp.where(empty & first_lane, MASKED, 0.0).astype(BF16)

    def queries_of(block):
        start, stop = block * QBLK, (block + 1) * QBLK
        unit = first_lane.astype(F32).astype(BF16)
        later = iota((QBLK, QBLK), 1) > iota((QBLK, QBLK), 0)
        ones = jnp.ones((stop, HEAD), BF16)
        for h in range(SHARE):
            q = jnp.concatenate([q_scr[h], unit], axis=1)
            k = jnp.concatenate([k_scr[h, 0:stop, :], mark_scr[0:stop, :]], axis=1)
            v = jnp.concatenate([v_scr[h, 0:stop, :], ones], axis=1)
            scores = lax.dot_general(
                q, k, (((1,), (1,)), ((), ())), preferred_element_type=F32
            )
            last = jnp.where(later, MASKED, scores[:, start:stop])
            if block:
                scores = jnp.concatenate([scores[:, :start], last], axis=1)
            else:
                scores = last
            top = jnp.max(scores, axis=1, keepdims=True)
            weights = jnp.exp2((scores - top) * FACTOR)
            mixed = dot(weights.astype(BF16), v)
            o_scr[h] = (mixed[:, :HEAD] / mixed[:, HEAD:]).astype(BF16)

    for block in range(ROWS // QBLK):
        pl.when(step == block)(lambda block=block: queries_of(block))

    for block in range(SOURCES // CHUNK):
        width = CHUNK * MOST
        tall = o_scr[:, block * width : (block + 1) * width, :].reshape(CHUNK * UNIT, HEAD)
        mixed = dot(scatter, tall).astype(BF16)
        out_ref[block * CHUNK : (block + 1) * CHUNK, :, :] = mixed.reshape(CHUNK, UNIT, HEAD)


def attend(received):
    held = pltpu.VMEM((SHARE, ROWS, HEAD), BF16)
    part = pltpu.VMEM((SHARE, QBLK, HEAD), BF16)
    return pl.pallas_call(
        attend_kernel,
        grid=(ROWS // QBLK,),
        in_specs=[pl.BlockSpec((SOURCES, 3 * UNIT, HEAD), lambda b: (b, 0, 0))],
        out_specs=pl.BlockSpec((SOURCES, UNIT, HEAD), lambda b: (b, 0, 0)),
        out_shape=jax.ShapeDtypeStruct((DEVICES, UNIT, HEAD), BF16),
        scratch_shapes=[held, held, part, part, pltpu.VMEM((ROWS, HEAD), BF16)],
        compiler_params=pltpu.CompilerParams(vmem_limit_bytes=VMEM),
        name="attend",
    )(received)


def unpack_kernel(row_ref, in_ref, out_ref):
    onehot = slot_onehot(row_ref[...]).astype(BF16)
    gather = spread_matrix(False)
    width = CHUNK * MOST
    blocks = []
    for block in range(CLUSTERS // CHUNK):
        tall = in_ref[block * CHUNK : (block + 1) * CHUNK, 0, :, :].reshape(CHUNK * UNIT, HEAD)
        mixed = dot(gather, tall).astype(BF16)
        blocks.append(
            jnp.concatenate([mixed[h * width : (h + 1) * width, :] for h in range(SHARE)], axis=1)
        )
    rows = jnp.concatenate(blocks, axis=0)
    out_ref[...] = lax.dot_general(
        onehot, rows, (((0,), (0,)), ((), ())), preferred_element_type=F32
    ).astype(BF16)


def unpack(row, back):
    return pl.pallas_call(
        unpack_kernel,
        grid=(GROUPS,),
        in_specs=[
            pl.BlockSpec((1, TOK), lambda g: (0, 0)),
            pl.BlockSpec((CLUSTERS, 1, UNIT, HEAD), lambda g: (0, g, 0, 0)),
        ],
        out_specs=pl.BlockSpec((TOK, SHARE * HEAD), lambda g: (0, g)),
        out_shape=jax.ShapeDtypeStruct((TOK, HEADS * HEAD), BF16),
        compiler_params=pltpu.CompilerParams(vmem_limit_bytes=VMEM),
        name="unpack",
    )(row, back)


def token_ranks(row):
    row = row.astype(F32)
    above, across = iota((TOK, TOK), 0), iota((TOK, TOK), 1)
    col = jnp.sum(jnp.where(above == across, row, 0.0), axis=1, keepdims=True)
    same = col == row
    second = jnp.sum((same & (above < across)).astype(F32), axis=0, keepdims=True)
    second_col = jnp.sum((same & (across < above)).astype(F32), axis=1, keepdims=True)
    group, group_col = jnp.floor(row / SHARE), jnp.floor(col / SHARE)
    lower = (second_col > 0.5) & (group_col == group) & (col < row)
    rank = jnp.sum(lower.astype(F32), axis=0, keepdims=True)
    return row, group, second, rank


def bits(mask):
    return mask.astype(F32).astype(BF16)


def lean_pack_kernel(row_ref, q_ref, k_ref, v_ref, out_ref):
    row, group, second, rank = token_ranks(row_ref[...])
    is_second = second > 0.5
    mine = iota((CLUSTERS, TOK), 0).astype(F32) == row
    first = mine & jnp.logical_not(is_second)
    filled = jnp.sum(first.astype(F32), axis=1, keepdims=True) > 0.5
    empty_entry = jnp.where(filled | (iota((1, HEAD), 1) > 0), 0.0, EMPTY)

    seconds = (mine & is_second).astype(F32)
    there = jnp.sum(seconds, axis=1, keepdims=True) > 0.5
    code = jnp.where(there, jnp.sum(seconds * rank, axis=1, keepdims=True), NONE)
    short = jnp.max(second * (rank + 1.0), axis=1, keepdims=True) > EXTRA + 0.5
    place, lane = iota((CLUSTERS, HEAD), 0) % SHARE, iota((CLUSTERS, HEAD), 1)
    codes = jnp.where(lane == place, code, 0.0)
    codes = jnp.where((lane == SHARE) & short, 1.0, codes).astype(BF16)
    size = CLUSTERS // SHARE * TAIL
    number = iota((size, CLUSTERS), 0)
    last = (number % TAIL == TAIL - 1) & (number // TAIL == iota((size, CLUSTERS), 1) // SHARE)
    notes = dot(bits(last), codes)

    fits = is_second & (rank < EXTRA - 0.5)
    slot = jnp.where(fits, group * TAIL + rank, -1000.0)
    number = number.astype(F32)
    chosen = jnp.concatenate([bits(number == slot + EXTRA * i) for i in range(3)], axis=1)
    data = [ref[...] for ref in (q_ref, k_ref, v_ref)]
    tail = dot(chosen, jnp.concatenate(data, axis=0))
    tail = tail + jnp.concatenate([notes] * SHARE, axis=1)
    q, k, v = [dot(bits(first), one) for one in data]
    k = k + jnp.concatenate([empty_entry] * SHARE, axis=1)
    for j in range(CLUSTERS // SHARE):
        rows = slice(j * SHARE, (j + 1) * SHARE)
        message = jnp.concatenate(
            [q[rows], k[rows], tail[j * TAIL : (j + 1) * TAIL], v[rows]], axis=0
        ).astype(BF16)
        for h in range(SHARE):
            out_ref[j, h] = message[:, h * HEAD : (h + 1) * HEAD]


def lean_pack(row, queries, keys, values):
    data = pl.BlockSpec((TOK, SHARE * HEAD), lambda g: (0, g))
    groups = CLUSTERS // SHARE
    return pl.pallas_call(
        lean_pack_kernel,
        grid=(GROUPS,),
        in_specs=[pl.BlockSpec((1, TOK), lambda g: (0, 0)), data, data, data],
        out_specs=pl.BlockSpec((groups, SHARE, MESSAGE, HEAD), lambda g: (0, g, 0, 0)),
        out_shape=jax.ShapeDtypeStruct((groups, HEADS, MESSAGE, HEAD), BF16),
        compiler_params=pltpu.CompilerParams(vmem_limit_bytes=VMEM),
        name="lean_pack",
    )(row, queries, keys, values)


def lean_attend_kernel(in_ref, out_ref, k_scr, v_scr, q_scr, o_scr, code_scr):
    step = pl.program_id(0)
    here = pl.multiple_of(step * QBLK, QBLK)
    size = SHARE * CHUNK
    row, col = iota((size, size), 0), iota((size, size), 1)
    turn = bits(col == row % CHUNK * SHARE + row // CHUNK)
    turn_back = bits(row == col % CHUNK * SHARE + col // CHUNK)
    lane = iota((size, HEAD), 1)
    own_lane = lane == iota((size, HEAD), 0) // CHUNK
    wide_row, wide_col = iota((size, CHUNK * TAIL), 0), iota((size, CHUNK * TAIL), 1)
    own_tail = wide_row % CHUNK == wide_col // TAIL
    pick_notes = bits(own_tail & (wide_col % TAIL == TAIL - 1))
    tail_place = jnp.where(own_tail, (wide_col % TAIL).astype(F32), -200.0)
    back_place = jnp.where(row % CHUNK == col // SHARE, (col % SHARE).astype(F32), -200.0)

    def keep(part, start, q, k, v):
        shape = (SHARE, CHUNK, HEAD)
        q_scr[:, part : part + CHUNK, :] = q.astype(BF16).reshape(shape)
        v_scr[:, pl.ds(start, CHUNK), :] = v.astype(BF16).reshape(shape)
        k_scr[:, pl.ds(start, CHUNK), :HEAD] = k.astype(BF16).reshape(shape)
        mark = jnp.where(k > EMPTY / 2, MASKED, 0.0)
        k_scr[:, pl.ds(start, CHUNK), HEAD:] = mark.astype(BF16).reshape(shape)

    for block in range(SOURCES // CHUNK):
        part = in_ref[block * CHUNK : (block + 1) * CHUNK, :, :].astype(F32)
        at = 2 * SHARE
        pieces = [part[:, :SHARE], part[:, SHARE:at], part[:, at + TAIL :]]
        tall = jnp.concatenate([one.reshape(size, HEAD) for one in pieces], axis=1)
        mixed = dot(turn, tall.astype(BF16))
        start = pl.multiple_of(here + block * CHUNK, CHUNK)
        keep(block * CHUNK, start, mixed[:, :HEAD], mixed[:, HEAD : 2 * HEAD], mixed[:, 2 * HEAD :])

        tail = part[:, at : at + TAIL].reshape(CHUNK * TAIL, HEAD).astype(BF16)
        notes = dot(pick_notes, tail)
        code = jnp.sum(jnp.where(own_lane, notes, 0.0), axis=1, keepdims=True)
        code_scr[block] = jnp.broadcast_to(code, (size, HEAD))
        chosen = jnp.concatenate([bits(tail_place == code + EXTRA * i) for i in range(3)], axis=0)
        found = dot(chosen, tail)
        k = found[size : 2 * size] + jnp.where((code < NONE / 2) & (lane == 0), EMPTY, 0.0)
        start = pl.multiple_of(here + SOURCES + block * CHUNK, CHUNK)
        keep(SOURCES + block * CHUNK, start, found[:size], k, found[2 * size :])

    def queries_of(block):
        start, stop = block * QBLK, (block + 1) * QBLK
        unit = bits(iota((QBLK, HEAD), 1) == 0)
        row, col = iota((QBLK, QBLK), 0), iota((QBLK, QBLK), 1)
        later = col % SOURCES * MOST + col // SOURCES > row % SOURCES * MOST + row // SOURCES
        ones = jnp.ones((stop, HEAD), BF16)
        for c in range(SHARE):
            q = jnp.concatenate([q_scr[c], unit], axis=1)
            v = jnp.concatenate([v_scr[c, 0:stop, :], ones], axis=1)
            scores = lax.dot_general(
                q, k_scr[c, 0:stop, :], (((1,), (1,)), ((), ())), preferred_element_type=F32
            )
            last = jnp.where(later, MASKED, scores[:, start:stop])
            if block:
                scores = jnp.concatenate([scores[:, :start], last], axis=1)
            else:
                scores = last
            top = jnp.max(scores, axis=1, keepdims=True)
            weights = jnp.exp2((scores - top) * FACTOR)
            mixed = dot(weights.astype(BF16), v)
            o_scr[c] = (mixed[:, :HEAD] / mixed[:, HEAD:]).astype(BF16)

    for block in range(ROWS // QBLK):
        pl.when(step == block)(lambda block=block: queries_of(block))

    for block in range(SOURCES // CHUNK):
        begin = block * CHUNK
        shape = (CHUNK, SHARE, HEAD)
        firsts = dot(turn_back, o_scr[:, begin : begin + CHUNK, :].reshape(size, HEAD))
        begin = begin + SOURCES
        chosen = bits(back_place == code_scr[block])
        seconds = lax.dot_general(
            chosen,
            o_scr[:, begin : begin + CHUNK, :].reshape(size, HEAD),
            (((0,), (0,)), ((), ())),
            preferred_element_type=F32,
        )
        both = jnp.concatenate([firsts.reshape(shape), seconds.reshape(shape)], axis=1)
        out_ref[block * CHUNK : (block + 1) * CHUNK, :, :] = both.astype(BF16)


def lean_attend(received):
    part = pltpu.VMEM((SHARE, QBLK, HEAD), BF16)
    return pl.pallas_call(
        lean_attend_kernel,
        grid=(ROWS // QBLK,),
        in_specs=[pl.BlockSpec((SOURCES, MESSAGE, HEAD), lambda b: (b, 0, 0))],
        out_specs=pl.BlockSpec((SOURCES, UNIT, HEAD), lambda b: (b, 0, 0)),
        out_shape=jax.ShapeDtypeStruct((DEVICES, UNIT, HEAD), BF16),
        scratch_shapes=[
            pltpu.VMEM((SHARE, ROWS, 2 * HEAD), BF16),
            pltpu.VMEM((SHARE, ROWS, HEAD), BF16),
            part,
            part,
            pltpu.VMEM((SOURCES // CHUNK, SHARE * CHUNK, HEAD), F32),
        ],
        compiler_params=pltpu.CompilerParams(vmem_limit_bytes=VMEM),
        name="lean_attend",
    )(received)


def lean_unpack_kernel(row_ref, in_ref, out_ref):
    row, group, second, rank = token_ranks(row_ref[...])
    slot = group * UNIT + jnp.where(second > 0.5, SHARE + rank, row - group * SHARE)
    onehot = bits(iota((CLUSTERS // SHARE * UNIT, TOK), 0).astype(F32) == slot)
    rows = jnp.concatenate(
        [
            jnp.concatenate([in_ref[j, h] for h in range(SHARE)], axis=1)
            for j in range(CLUSTERS // SHARE)
        ],
        axis=0,
    )
    out_ref[...] = lax.dot_general(
        onehot, rows, (((0,), (0,)), ((), ())), preferred_element_type=F32
    ).astype(BF16)


def lean_unpack(row, back):
    groups = CLUSTERS // SHARE
    return pl.pallas_call(
        lean_unpack_kernel,
        grid=(GROUPS,),
        in_specs=[
            pl.BlockSpec((1, TOK), lambda g: (0, 0)),
            pl.BlockSpec((groups, SHARE, UNIT, HEAD), lambda g: (0, g, 0, 0)),
        ],
        out_specs=pl.BlockSpec((TOK, SHARE * HEAD), lambda g: (0, g)),
        out_shape=jax.ShapeDtypeStruct((TOK, HEADS * HEAD), BF16),
        compiler_params=pltpu.CompilerParams(vmem_limit_bytes=VMEM),
        name="lean_unpack",
    )(row, back)


def exchange(data):
    return lax.all_to_all(data, ("seq", "blk"), split_axis=0, concat_axis=0, tiled=True)


def body(queries, keys, values, cluster_ids):
    row = cluster_ids.reshape(1, TOK)
    sent = lean_pack(row, queries, keys, values)
    received = exchange(sent.reshape(DEVICES, MESSAGE, HEAD))
    short = jnp.max(received[:, 2 * SHARE + TAIL - 1, SHARE]) > 0

    def lean(received, row, queries, keys, values):
        back = exchange(lean_attend(received))
        return lean_unpack(row, back.reshape(CLUSTERS // SHARE, HEADS, UNIT, HEAD))

    def full(received, row, queries, keys, values):
        sent = pack(row, queries, keys, values)
        back = exchange(attend(exchange(sent.reshape(DEVICES, 3 * UNIT, HEAD))))
        return unpack(row, back.reshape(CLUSTERS, GROUPS, UNIT, HEAD))

    return lax.cond(short, full, lean, received, row, queries, keys, values)


def solution(mesh):
    spec = P(("seq", "blk"), None)
    return jax.shard_map(
        body, mesh=mesh, in_specs=(spec,) * 4, out_specs=spec, check_vma=False
    )
```

```python
import jax
import jax.numpy as jnp
from jax import lax
from jax.experimental import pallas as pl
from jax.experimental.pallas import tpu as pltpu
from jax.sharding import PartitionSpec as P

HEADS = 32
HEAD = 128
TOK = 128
CLUSTERS = 128
MOST = 2
GROUPS = 4
SHARE = HEADS // GROUPS
UNIT = SHARE * MOST
DEVICES = CLUSTERS * GROUPS
ROWS = DEVICES * MOST
QBLK = 256
SOURCES = QBLK // MOST
CHUNK = 16
VMEM = 56 * 1024 * 1024
EXTRA = 5
TAIL = 16
MESSAGE = 3 * SHARE + TAIL
NONE = -64.0
EMPTY = 256.0
MASKED = -1e30
FACTOR = 1.4426950408889634 / HEAD**0.5
BF16 = jnp.bfloat16
F32 = jnp.float32


def iota(shape, dim):
    return lax.broadcasted_iota(jnp.int32, shape, dim)


def spread_matrix(inverse):
    size = CHUNK * UNIT
    out, src = iota((size, size), 0), iota((size, size), 1)
    if inverse:
        out, src = src, out
    h, d, s = out // (CHUNK * MOST), (out // MOST) % CHUNK, out % MOST
    return (src == d * UNIT + h * MOST + s).astype(F32).astype(BF16)


def slot_onehot(row):
    row = row.astype(F32)
    above, across = iota((TOK, TOK), 0), iota((TOK, TOK), 1)
    col = jnp.sum(jnp.where(above == across, row, 0.0), axis=1, keepdims=True)
    earlier = (col == row) & (above < across)
    slots = row * MOST + jnp.sum(earlier.astype(F32), axis=0, keepdims=True)
    return (iota((CLUSTERS * MOST, TOK), 0).astype(F32) == slots).astype(F32)


def dot(a, b):
    return jnp.dot(a, b, preferred_element_type=F32)


def pack_kernel(row_ref, q_ref, k_ref, v_ref, out_ref):
    onehot = slot_onehot(row_ref[...])
    filled = jnp.sum(onehot, axis=1, keepdims=True) > 0.5
    onehot = onehot.astype(BF16)
    empty_entry = jnp.where(filled | (iota((1, HEAD), 1) > 0), 0.0, EMPTY)
    empty_entry = jnp.concatenate([empty_entry] * SHARE, axis=1)
    scatter = spread_matrix(True)
    rows = [dot(onehot, ref[...]) for ref in (q_ref, k_ref, v_ref)]
    rows[1] = rows[1] + empty_entry
    rows = [one.astype(BF16) for one in rows]
    width = CHUNK * MOST
    for block in range(CLUSTERS // CHUNK):
        tall = jnp.concatenate(
            [
                jnp.concatenate(
                    [
                        one[block * width : (block + 1) * width, h * HEAD : (h + 1) * HEAD]
                        for h in range(SHARE)
                    ],
                    axis=0,
                )
                for one in rows
            ],
            axis=1,
        )
        mixed = dot(scatter, tall).astype(BF16)
        for index in range(3):
            out_ref[
                block * CHUNK : (block + 1) * CHUNK, 0, index * UNIT : (index + 1) * UNIT, :
            ] = mixed[:, index * HEAD : (index + 1) * HEAD].reshape(CHUNK, UNIT, HEAD)


def pack(row, queries, keys, values):
    data = pl.BlockSpec((TOK, SHARE * HEAD), lambda g: (0, g))
    return pl.pallas_call(
        pack_kernel,
        grid=(GROUPS,),
        in_specs=[pl.BlockSpec((1, TOK), lambda g: (0, 0)), data, data, data],
        out_specs=pl.BlockSpec((CLUSTERS, 1, 3 * UNIT, HEAD), lambda g: (0, g, 0, 0)),
        out_shape=jax.ShapeDtypeStruct((CLUSTERS, GROUPS, 3 * UNIT, HEAD), BF16),
        compiler_params=pltpu.CompilerParams(vmem_limit_bytes=VMEM),
        name="pack",
    )(row, queries, keys, values)


def attend_kernel(in_ref, out_ref, k_scr, v_scr, q_scr, o_scr, mark_scr):
    step = pl.program_id(0)
    gather, scatter = spread_matrix(False), spread_matrix(True)
    first_lane = iota((QBLK, HEAD), 1) == 0

    def regroup(block):
        part = in_ref[block * CHUNK : (block + 1) * CHUNK, :, :]
        tall = jnp.concatenate(
            [
                part[:, i * UNIT : (i + 1) * UNIT, :].reshape(CHUNK * UNIT, HEAD)
                for i in range(3)
            ],
            axis=1,
        )
        mixed = dot(gather, tall).astype(BF16)
        width = CHUNK * MOST
        start = pl.multiple_of(step * QBLK + block * width, width)
        q_scr[:, block * width : (block + 1) * width, :] = mixed[:, :HEAD].reshape(
            SHARE, width, HEAD
        )
        k_scr[:, pl.ds(start, width), :] = mixed[:, HEAD : 2 * HEAD].reshape(SHARE, width, HEAD)
        v_scr[:, pl.ds(start, width), :] = mixed[:, 2 * HEAD :].reshape(SHARE, width, HEAD)

    for block in range(SOURCES // CHUNK):
        regroup(block)

    here = pl.multiple_of(step * QBLK, QBLK)
    empty = k_scr[0, pl.ds(here, QBLK), :].astype(F32) > EMPTY / 2
    mark_scr[pl.ds(here, QBLK), :] = jnp.where(empty & first_lane, MASKED, 0.0).astype(BF16)

    def queries_of(block):
        start, stop = block * QBLK, (block + 1) * QBLK
        unit = first_lane.astype(F32).astype(BF16)
        later = iota((QBLK, QBLK), 1) > iota((QBLK, QBLK), 0)
        ones = jnp.ones((stop, HEAD), BF16)
        for h in range(SHARE):
            q = jnp.concatenate([q_scr[h], unit], axis=1)
            k = jnp.concatenate([k_scr[h, 0:stop, :], mark_scr[0:stop, :]], axis=1)
            v = jnp.concatenate([v_scr[h, 0:stop, :], ones], axis=1)
            scores = lax.dot_general(
                q, k, (((1,), (1,)), ((), ())), preferred_element_type=F32
            )
            last = jnp.where(later, MASKED, scores[:, start:stop])
            if block:
                scores = jnp.concatenate([scores[:, :start], last], axis=1)
            else:
                scores = last
            top = jnp.max(scores, axis=1, keepdims=True)
            weights = jnp.exp2((scores - top) * FACTOR)
            mixed = dot(weights.astype(BF16), v)
            o_scr[h] = (mixed[:, :HEAD] / mixed[:, HEAD:]).astype(BF16)

    for block in range(ROWS // QBLK):
        pl.when(step == block)(lambda block=block: queries_of(block))

    for block in range(SOURCES // CHUNK):
        width = CHUNK * MOST
        tall = o_scr[:, block * width : (block + 1) * width, :].reshape(CHUNK * UNIT, HEAD)
        mixed = dot(scatter, tall).astype(BF16)
        out_ref[block * CHUNK : (block + 1) * CHUNK, :, :] = mixed.reshape(CHUNK, UNIT, HEAD)


def attend(received):
    held = pltpu.VMEM((SHARE, ROWS, HEAD), BF16)
    part = pltpu.VMEM((SHARE, QBLK, HEAD), BF16)
    return pl.pallas_call(
        attend_kernel,
        grid=(ROWS // QBLK,),
        in_specs=[pl.BlockSpec((SOURCES, 3 * UNIT, HEAD), lambda b: (b, 0, 0))],
        out_specs=pl.BlockSpec((SOURCES, UNIT, HEAD), lambda b: (b, 0, 0)),
        out_shape=jax.ShapeDtypeStruct((DEVICES, UNIT, HEAD), BF16),
        scratch_shapes=[held, held, part, part, pltpu.VMEM((ROWS, HEAD), BF16)],
        compiler_params=pltpu.CompilerParams(vmem_limit_bytes=VMEM),
        name="attend",
    )(received)


def unpack_kernel(row_ref, in_ref, out_ref):
    onehot = slot_onehot(row_ref[...]).astype(BF16)
    gather = spread_matrix(False)
    width = CHUNK * MOST
    blocks = []
    for block in range(CLUSTERS // CHUNK):
        tall = in_ref[block * CHUNK : (block + 1) * CHUNK, 0, :, :].reshape(CHUNK * UNIT, HEAD)
        mixed = dot(gather, tall).astype(BF16)
        blocks.append(
            jnp.concatenate([mixed[h * width : (h + 1) * width, :] for h in range(SHARE)], axis=1)
        )
    rows = jnp.concatenate(blocks, axis=0)
    out_ref[...] = lax.dot_general(
        onehot, rows, (((0,), (0,)), ((), ())), preferred_element_type=F32
    ).astype(BF16)


def unpack(row, back):
    return pl.pallas_call(
        unpack_kernel,
        grid=(GROUPS,),
        in_specs=[
            pl.BlockSpec((1, TOK), lambda g: (0, 0)),
            pl.BlockSpec((CLUSTERS, 1, UNIT, HEAD), lambda g: (0, g, 0, 0)),
        ],
        out_specs=pl.BlockSpec((TOK, SHARE * HEAD), lambda g: (0, g)),
        out_shape=jax.ShapeDtypeStruct((TOK, HEADS * HEAD), BF16),
        compiler_params=pltpu.CompilerParams(vmem_limit_bytes=VMEM),
        name="unpack",
    )(row, back)


def token_ranks(row):
    row = row.astype(F32)
    above, across = iota((TOK, TOK), 0), iota((TOK, TOK), 1)
    col = jnp.sum(jnp.where(above == across, row, 0.0), axis=1, keepdims=True)
    same = col == row
    second = jnp.sum((same & (above < across)).astype(F32), axis=0, keepdims=True)
    second_col = jnp.sum((same & (across < above)).astype(F32), axis=1, keepdims=True)
    group, group_col = jnp.floor(row / SHARE), jnp.floor(col / SHARE)
    lower = (second_col > 0.5) & (group_col == group) & (col < row)
    rank = jnp.sum(lower.astype(F32), axis=0, keepdims=True)
    return row, group, second, rank


def bits(mask):
    return mask.astype(F32).astype(BF16)


def lean_pack_kernel(
    row_ref, q_ref, k_ref, v_ref, out_ref, first_scr, empty_scr, notes_scr, chosen_scr
):
    @pl.when(pl.program_id(0) == 0)
    def prepare():
        row, group, second, rank = token_ranks(row_ref[...])
        is_second = second > 0.5
        mine = iota((CLUSTERS, TOK), 0).astype(F32) == row
        first = mine & jnp.logical_not(is_second)
        first_scr[...] = bits(first)
        filled = jnp.sum(first.astype(F32), axis=1, keepdims=True) > 0.5
        empty_scr[...] = jnp.where(filled | (iota((1, HEAD), 1) > 0), 0.0, EMPTY)

        seconds = (mine & is_second).astype(F32)
        there = jnp.sum(seconds, axis=1, keepdims=True) > 0.5
        code = jnp.where(there, jnp.sum(seconds * rank, axis=1, keepdims=True), NONE)
        short = jnp.max(second * (rank + 1.0), axis=1, keepdims=True) > EXTRA + 0.5
        place, lane = iota((CLUSTERS, HEAD), 0) % SHARE, iota((CLUSTERS, HEAD), 1)
        codes = jnp.where(lane == place, code, 0.0)
        codes = jnp.where((lane == SHARE) & short, 1.0, codes).astype(BF16)
        size = CLUSTERS // SHARE * TAIL
        number = iota((size, CLUSTERS), 0)
        last = (number % TAIL == TAIL - 1) & (number // TAIL == iota((size, CLUSTERS), 1) // SHARE)
        notes_scr[...] = dot(bits(last), codes)

        fits = is_second & (rank < EXTRA - 0.5)
        slot = jnp.where(fits, group * TAIL + rank, -1000.0)
        number = number.astype(F32)
        chosen_scr[...] = jnp.concatenate(
            [bits(number == slot + EXTRA * i) for i in range(3)], axis=1
        )

    data = [ref[...] for ref in (q_ref, k_ref, v_ref)]
    tail = dot(chosen_scr[...], jnp.concatenate(data, axis=0))
    tail = tail + jnp.concatenate([notes_scr[...]] * SHARE, axis=1)
    q, k, v = [dot(first_scr[...], one) for one in data]
    k = k + jnp.concatenate([empty_scr[...]] * SHARE, axis=1)
    for j in range(CLUSTERS // SHARE):
        rows = slice(j * SHARE, (j + 1) * SHARE)
        message = jnp.concatenate(
            [q[rows], k[rows], tail[j * TAIL : (j + 1) * TAIL], v[rows]], axis=0
        ).astype(BF16)
        for h in range(SHARE):
            out_ref[j, h] = message[:, h * HEAD : (h + 1) * HEAD]


def lean_pack(row, queries, keys, values):
    data = pl.BlockSpec((TOK, SHARE * HEAD), lambda g: (0, g))
    groups = CLUSTERS // SHARE
    return pl.pallas_call(
        lean_pack_kernel,
        grid=(GROUPS,),
        in_specs=[pl.BlockSpec((1, TOK), lambda g: (0, 0)), data, data, data],
        out_specs=pl.BlockSpec((groups, SHARE, MESSAGE, HEAD), lambda g: (0, g, 0, 0)),
        out_shape=jax.ShapeDtypeStruct((groups, HEADS, MESSAGE, HEAD), BF16),
        scratch_shapes=[
            pltpu.VMEM((CLUSTERS, TOK), BF16),
            pltpu.VMEM((CLUSTERS, HEAD), F32),
            pltpu.VMEM((groups * TAIL, HEAD), F32),
            pltpu.VMEM((groups * TAIL, 3 * TOK), BF16),
        ],
        compiler_params=pltpu.CompilerParams(vmem_limit_bytes=VMEM),
        name="lean_pack",
    )(row, queries, keys, values)


def lean_attend_kernel(in_ref, out_ref, flag_ref, k_scr, v_scr, q_scr, o_scr, code_scr):
    step = pl.program_id(0)
    size = SHARE * CHUNK
    row, col = iota((size, size), 0), iota((size, size), 1)
    turn = bits(col == row % CHUNK * SHARE + row // CHUNK)
    turn_back = bits(row == col % CHUNK * SHARE + col // CHUNK)
    lane = iota((size, HEAD), 1)
    own_lane = lane == iota((size, HEAD), 0) // CHUNK
    wide_row, wide_col = iota((size, CHUNK * TAIL), 0), iota((size, CHUNK * TAIL), 1)
    own_tail = wide_row % CHUNK == wide_col // TAIL
    pick_notes = bits(own_tail & (wide_col % TAIL == TAIL - 1))
    tail_place = jnp.where(own_tail, (wide_col % TAIL).astype(F32), -200.0)
    back_place = jnp.where(row % CHUNK == col // SHARE, (col % SHARE).astype(F32), -200.0)

    def keep(part, start, q, k, v):
        shape = (SHARE, CHUNK, HEAD)
        q_scr[:, part : part + CHUNK, :] = q.astype(BF16).reshape(shape)
        v_scr[:, start : start + CHUNK, :] = v.astype(BF16).reshape(shape)
        k_scr[:, start : start + CHUNK, :HEAD] = k.astype(BF16).reshape(shape)
        mark = jnp.where(k > EMPTY / 2, MASKED, 0.0)
        k_scr[:, start : start + CHUNK, HEAD:] = mark.astype(BF16).reshape(shape)

    def load_all(here):
        flags = jnp.zeros((size, HEAD), F32)
        for block in range(SOURCES // CHUNK):
            part = in_ref[block * CHUNK : (block + 1) * CHUNK, :, :].astype(F32)
            at = 2 * SHARE
            pieces = [part[:, :SHARE], part[:, SHARE:at], part[:, at + TAIL :]]
            tall = jnp.concatenate([one.reshape(size, HEAD) for one in pieces], axis=1)
            mixed = dot(turn, tall.astype(BF16))
            start = here + block * CHUNK
            keep(block * CHUNK, start, mixed[:, :HEAD], mixed[:, HEAD : 2 * HEAD], mixed[:, 2 * HEAD :])

            tail = part[:, at : at + TAIL].reshape(CHUNK * TAIL, HEAD).astype(BF16)
            notes = dot(pick_notes, tail)
            flags = jnp.maximum(flags, notes)
            code = jnp.sum(jnp.where(own_lane, notes, 0.0), axis=1, keepdims=True)
            code_scr[block] = jnp.broadcast_to(code, (size, HEAD))
            chosen = jnp.concatenate([bits(tail_place == code + EXTRA * i) for i in range(3)], axis=0)
            found = dot(chosen, tail)
            k = found[size : 2 * size] + jnp.where((code < NONE / 2) & (lane == 0), EMPTY, 0.0)
            start = here + SOURCES + block * CHUNK
            keep(SOURCES + block * CHUNK, start, found[:size], k, found[2 * size :])

        flags = jnp.max(flags, axis=0, keepdims=True)
        if here:
            flags = jnp.maximum(flags, flag_ref[0:1, :])
        flag_ref[...] = jnp.broadcast_to(flags, flag_ref.shape)

    def queries_of(block):
        start, stop = block * QBLK, (block + 1) * QBLK
        unit = bits(iota((QBLK, HEAD), 1) == 0)
        row, col = iota((QBLK, 1), 0), iota((1, QBLK), 1)
        row, col = [one % SOURCES * MOST + one // SOURCES for one in (row, col)]
        later = col > row
        ones = jnp.ones((stop, HEAD), BF16)
        for c in range(SHARE):
            q = jnp.concatenate([q_scr[c], unit], axis=1)
            v = jnp.concatenate([v_scr[c, 0:stop, :], ones], axis=1)
            scores = lax.dot_general(
                q, k_scr[c, 0:stop, :], (((1,), (1,)), ((), ())), preferred_element_type=F32
            )
            last = jnp.where(later, MASKED, scores[:, start:stop])
            if block:
                scores = jnp.concatenate([scores[:, :start], last], axis=1)
            else:
                scores = last
            top = jnp.max(scores, axis=1, keepdims=True)
            weights = jnp.exp2((scores - top) * FACTOR)
            mixed = dot(weights.astype(BF16), v)
            o_scr[c] = (mixed[:, :HEAD] / mixed[:, HEAD:]).astype(BF16)

    def store_all():
        for block in range(SOURCES // CHUNK):
            begin = block * CHUNK
            shape = (CHUNK, SHARE, HEAD)
            firsts = dot(turn_back, o_scr[:, begin : begin + CHUNK, :].reshape(size, HEAD))
            begin = begin + SOURCES
            chosen = bits(back_place == code_scr[block])
            seconds = lax.dot_general(
                chosen,
                o_scr[:, begin : begin + CHUNK, :].reshape(size, HEAD),
                (((0,), (0,)), ((), ())),
                preferred_element_type=F32,
            )
            both = jnp.concatenate([firsts.reshape(shape), seconds.reshape(shape)], axis=1)
            out_ref[block * CHUNK : (block + 1) * CHUNK, :, :] = both.astype(BF16)

    def work(number):
        load_all(number * QBLK)
        queries_of(number)
        store_all()

    for block in range(ROWS // QBLK):
        pl.when(step == block)(lambda block=block: work(block))


def lean_attend(received):
    part = pltpu.VMEM((SHARE, QBLK, HEAD), BF16)
    return pl.pallas_call(
        lean_attend_kernel,
        grid=(ROWS // QBLK,),
        in_specs=[pl.BlockSpec((SOURCES, MESSAGE, HEAD), lambda b: (b, 0, 0))],
        out_specs=[
            pl.BlockSpec((SOURCES, UNIT, HEAD), lambda b: (b, 0, 0)),
            pl.BlockSpec((8, HEAD), lambda b: (0, 0)),
        ],
        out_shape=[
            jax.ShapeDtypeStruct((DEVICES, UNIT, HEAD), BF16),
            jax.ShapeDtypeStruct((8, HEAD), F32),
        ],
        scratch_shapes=[
            pltpu.VMEM((SHARE, ROWS, 2 * HEAD), BF16),
            pltpu.VMEM((SHARE, ROWS, HEAD), BF16),
            part,
            part,
            pltpu.VMEM((SOURCES // CHUNK, SHARE * CHUNK, HEAD), F32),
        ],
        compiler_params=pltpu.CompilerParams(vmem_limit_bytes=VMEM),
        name="lean_attend",
    )(received)


def lean_unpack_kernel(row_ref, in_ref, out_ref, onehot_scr):
    @pl.when(pl.program_id(0) == 0)
    def prepare():
        row, group, second, rank = token_ranks(row_ref[...])
        slot = group * UNIT + jnp.where(second > 0.5, SHARE + rank, row - group * SHARE)
        onehot_scr[...] = bits(iota(onehot_scr.shape, 0).astype(F32) == slot)

    rows = jnp.concatenate(
        [
            jnp.concatenate([in_ref[j, h] for h in range(SHARE)], axis=1)
            for j in range(CLUSTERS // SHARE)
        ],
        axis=0,
    )
    out_ref[...] = lax.dot_general(
        onehot_scr[...], rows, (((0,), (0,)), ((), ())), preferred_element_type=F32
    ).astype(BF16)


def lean_unpack(row, back):
    groups = CLUSTERS // SHARE
    return pl.pallas_call(
        lean_unpack_kernel,
        grid=(GROUPS,),
        in_specs=[
            pl.BlockSpec((1, TOK), lambda g: (0, 0)),
            pl.BlockSpec((groups, SHARE, UNIT, HEAD), lambda g: (0, g, 0, 0)),
        ],
        out_specs=pl.BlockSpec((TOK, SHARE * HEAD), lambda g: (0, g)),
        out_shape=jax.ShapeDtypeStruct((TOK, HEADS * HEAD), BF16),
        scratch_shapes=[pltpu.VMEM((groups * UNIT, TOK), BF16)],
        compiler_params=pltpu.CompilerParams(vmem_limit_bytes=63 * 1024 * 1024),
        name="lean_unpack",
    )(row, back)


def exchange(data):
    return lax.all_to_all(data, ("seq", "blk"), split_axis=0, concat_axis=0, tiled=True)


def body(queries, keys, values, cluster_ids):
    row = cluster_ids.reshape(1, TOK)
    sent = lean_pack(row, queries, keys, values)
    received = exchange(sent.reshape(DEVICES, MESSAGE, HEAD))
    mixed, flags = lean_attend(received)
    back = exchange(mixed)
    short = flags[0, SHARE] > 0.5

    def lean(back, row, queries, keys, values):
        return lean_unpack(row, back.reshape(CLUSTERS // SHARE, HEADS, UNIT, HEAD))

    def full(back, row, queries, keys, values):
        sent = pack(row, queries, keys, values)
        back = exchange(attend(exchange(sent.reshape(DEVICES, 3 * UNIT, HEAD))))
        return unpack(row, back.reshape(CLUSTERS, GROUPS, UNIT, HEAD))

    return lax.cond(short, full, lean, back, row, queries, keys, values)


def solution(mesh):
    spec = P(("seq", "blk"), None)
    return jax.shard_map(
        body, mesh=mesh, in_specs=(spec,) * 4, out_specs=spec, check_vma=False
    )
```

```python
import jax
import jax.numpy as jnp
from jax import lax
from jax.experimental import pallas as pl
from jax.experimental.pallas import tpu as pltpu
from jax.sharding import PartitionSpec as P

HEADS = 32
HEAD = 128
TOK = 128
CLUSTERS = 128
MOST = 2
GROUPS = 4
SHARE = HEADS // GROUPS
UNIT = SHARE * MOST
DEVICES = CLUSTERS * GROUPS
ROWS = DEVICES * MOST
QBLK = 256
SOURCES = QBLK // MOST
CHUNK = 16
VMEM = 56 * 1024 * 1024
PAIR = 2
POOL = PAIR * SHARE
EXTRA = 5
TAIL = 16
HALF = TAIL // PAIR
MESSAGE = 3 * SHARE + HALF
CHIPS = 4
NONE = -64.0
EMPTY = 256.0
MASKED = -1e30
FACTOR = 1.4426950408889634 / HEAD**0.5
BF16 = jnp.bfloat16
F32 = jnp.float32


def iota(shape, dim):
    return lax.broadcasted_iota(jnp.int32, shape, dim)


def spread_matrix(inverse):
    size = CHUNK * UNIT
    out, src = iota((size, size), 0), iota((size, size), 1)
    if inverse:
        out, src = src, out
    h, d, s = out // (CHUNK * MOST), (out // MOST) % CHUNK, out % MOST
    return (src == d * UNIT + h * MOST + s).astype(F32).astype(BF16)


def slot_onehot(row):
    row = row.astype(F32)
    above, across = iota((TOK, TOK), 0), iota((TOK, TOK), 1)
    col = jnp.sum(jnp.where(above == across, row, 0.0), axis=1, keepdims=True)
    earlier = (col == row) & (above < across)
    slots = row * MOST + jnp.sum(earlier.astype(F32), axis=0, keepdims=True)
    return (iota((CLUSTERS * MOST, TOK), 0).astype(F32) == slots).astype(F32)


def dot(a, b):
    return jnp.dot(a, b, preferred_element_type=F32)


def pack_kernel(row_ref, q_ref, k_ref, v_ref, out_ref):
    onehot = slot_onehot(row_ref[...])
    filled = jnp.sum(onehot, axis=1, keepdims=True) > 0.5
    onehot = onehot.astype(BF16)
    empty_entry = jnp.where(filled | (iota((1, HEAD), 1) > 0), 0.0, EMPTY)
    empty_entry = jnp.concatenate([empty_entry] * SHARE, axis=1)
    scatter = spread_matrix(True)
    rows = [dot(onehot, ref[...]) for ref in (q_ref, k_ref, v_ref)]
    rows[1] = rows[1] + empty_entry
    rows = [one.astype(BF16) for one in rows]
    width = CHUNK * MOST
    for block in range(CLUSTERS // CHUNK):
        tall = jnp.concatenate(
            [
                jnp.concatenate(
                    [
                        one[block * width : (block + 1) * width, h * HEAD : (h + 1) * HEAD]
                        for h in range(SHARE)
                    ],
                    axis=0,
                )
                for one in rows
            ],
            axis=1,
        )
        mixed = dot(scatter, tall).astype(BF16)
        for index in range(3):
            out_ref[
                block * CHUNK : (block + 1) * CHUNK, 0, index * UNIT : (index + 1) * UNIT, :
            ] = mixed[:, index * HEAD : (index + 1) * HEAD].reshape(CHUNK, UNIT, HEAD)


def pack(row, queries, keys, values):
    data = pl.BlockSpec((TOK, SHARE * HEAD), lambda g: (0, g))
    return pl.pallas_call(
        pack_kernel,
        grid=(GROUPS,),
        in_specs=[pl.BlockSpec((1, TOK), lambda g: (0, 0)), data, data, data],
        out_specs=pl.BlockSpec((CLUSTERS, 1, 3 * UNIT, HEAD), lambda g: (0, g, 0, 0)),
        out_shape=jax.ShapeDtypeStruct((CLUSTERS, GROUPS, 3 * UNIT, HEAD), BF16),
        compiler_params=pltpu.CompilerParams(vmem_limit_bytes=VMEM),
        name="pack",
    )(row, queries, keys, values)


def attend_kernel(in_ref, out_ref, k_scr, v_scr, q_scr, o_scr, mark_scr):
    step = pl.program_id(0)
    gather, scatter = spread_matrix(False), spread_matrix(True)
    first_lane = iota((QBLK, HEAD), 1) == 0

    def regroup(block):
        part = in_ref[block * CHUNK : (block + 1) * CHUNK, :, :]
        tall = jnp.concatenate(
            [
                part[:, i * UNIT : (i + 1) * UNIT, :].reshape(CHUNK * UNIT, HEAD)
                for i in range(3)
            ],
            axis=1,
        )
        mixed = dot(gather, tall).astype(BF16)
        width = CHUNK * MOST
        start = pl.multiple_of(step * QBLK + block * width, width)
        q_scr[:, block * width : (block + 1) * width, :] = mixed[:, :HEAD].reshape(
            SHARE, width, HEAD
        )
        k_scr[:, pl.ds(start, width), :] = mixed[:, HEAD : 2 * HEAD].reshape(SHARE, width, HEAD)
        v_scr[:, pl.ds(start, width), :] = mixed[:, 2 * HEAD :].reshape(SHARE, width, HEAD)

    for block in range(SOURCES // CHUNK):
        regroup(block)

    here = pl.multiple_of(step * QBLK, QBLK)
    empty = k_scr[0, pl.ds(here, QBLK), :].astype(F32) > EMPTY / 2
    mark_scr[pl.ds(here, QBLK), :] = jnp.where(empty & first_lane, MASKED, 0.0).astype(BF16)

    def queries_of(block):
        start, stop = block * QBLK, (block + 1) * QBLK
        unit = first_lane.astype(F32).astype(BF16)
        later = iota((QBLK, QBLK), 1) > iota((QBLK, QBLK), 0)
        ones = jnp.ones((stop, HEAD), BF16)
        for h in range(SHARE):
            q = jnp.concatenate([q_scr[h], unit], axis=1)
            k = jnp.concatenate([k_scr[h, 0:stop, :], mark_scr[0:stop, :]], axis=1)
            v = jnp.concatenate([v_scr[h, 0:stop, :], ones], axis=1)
            scores = lax.dot_general(
                q, k, (((1,), (1,)), ((), ())), preferred_element_type=F32
            )
            last = jnp.where(later, MASKED, scores[:, start:stop])
            if block:
                scores = jnp.concatenate([scores[:, :start], last], axis=1)
            else:
                scores = last
            top = jnp.max(scores, axis=1, keepdims=True)
            weights = jnp.exp2((scores - top) * FACTOR)
            mixed = dot(weights.astype(BF16), v)
            o_scr[h] = (mixed[:, :HEAD] / mixed[:, HEAD:]).astype(BF16)

    for block in range(ROWS // QBLK):
        pl.when(step == block)(lambda block=block: queries_of(block))

    for block in range(SOURCES // CHUNK):
        width = CHUNK * MOST
        tall = o_scr[:, block * width : (block + 1) * width, :].reshape(CHUNK * UNIT, HEAD)
        mixed = dot(scatter, tall).astype(BF16)
        out_ref[block * CHUNK : (block + 1) * CHUNK, :, :] = mixed.reshape(CHUNK, UNIT, HEAD)


def attend(received):
    held = pltpu.VMEM((SHARE, ROWS, HEAD), BF16)
    part = pltpu.VMEM((SHARE, QBLK, HEAD), BF16)
    return pl.pallas_call(
        attend_kernel,
        grid=(ROWS // QBLK,),
        in_specs=[pl.BlockSpec((SOURCES, 3 * UNIT, HEAD), lambda b: (b, 0, 0))],
        out_specs=pl.BlockSpec((SOURCES, UNIT, HEAD), lambda b: (b, 0, 0)),
        out_shape=jax.ShapeDtypeStruct((DEVICES, UNIT, HEAD), BF16),
        scratch_shapes=[held, held, part, part, pltpu.VMEM((ROWS, HEAD), BF16)],
        compiler_params=pltpu.CompilerParams(vmem_limit_bytes=VMEM),
        name="attend",
    )(received)


def unpack_kernel(row_ref, in_ref, out_ref):
    onehot = slot_onehot(row_ref[...]).astype(BF16)
    gather = spread_matrix(False)
    width = CHUNK * MOST
    blocks = []
    for block in range(CLUSTERS // CHUNK):
        tall = in_ref[block * CHUNK : (block + 1) * CHUNK, 0, :, :].reshape(CHUNK * UNIT, HEAD)
        mixed = dot(gather, tall).astype(BF16)
        blocks.append(
            jnp.concatenate([mixed[h * width : (h + 1) * width, :] for h in range(SHARE)], axis=1)
        )
    rows = jnp.concatenate(blocks, axis=0)
    out_ref[...] = lax.dot_general(
        onehot, rows, (((0,), (0,)), ((), ())), preferred_element_type=F32
    ).astype(BF16)


def unpack(row, back):
    return pl.pallas_call(
        unpack_kernel,
        grid=(GROUPS,),
        in_specs=[
            pl.BlockSpec((1, TOK), lambda g: (0, 0)),
            pl.BlockSpec((CLUSTERS, 1, UNIT, HEAD), lambda g: (0, g, 0, 0)),
        ],
        out_specs=pl.BlockSpec((TOK, SHARE * HEAD), lambda g: (0, g)),
        out_shape=jax.ShapeDtypeStruct((TOK, HEADS * HEAD), BF16),
        compiler_params=pltpu.CompilerParams(vmem_limit_bytes=VMEM),
        name="unpack",
    )(row, back)


def token_ranks(row):
    row = row.astype(F32)
    above, across = iota((TOK, TOK), 0), iota((TOK, TOK), 1)
    col = jnp.sum(jnp.where(above == across, row, 0.0), axis=1, keepdims=True)
    same = col == row
    second = jnp.sum((same & (above < across)).astype(F32), axis=0, keepdims=True)
    second_col = jnp.sum((same & (across < above)).astype(F32), axis=1, keepdims=True)
    group, group_col = jnp.floor(row / POOL), jnp.floor(col / POOL)
    lower = (second_col > 0.5) & (group_col == group) & (col < row)
    rank = jnp.sum(lower.astype(F32), axis=0, keepdims=True)
    return row, group, second, rank


def bits(mask):
    return mask.astype(F32).astype(BF16)


def lean_pack_kernel(
    row_ref, q_ref, k_ref, v_ref, out_ref, first_scr, empty_scr, notes_scr, chosen_scr
):
    @pl.when(pl.program_id(0) == 0)
    def prepare():
        row, group, second, rank = token_ranks(row_ref[...])
        is_second = second > 0.5
        mine = iota((CLUSTERS, TOK), 0).astype(F32) == row
        first = mine & jnp.logical_not(is_second)
        first_scr[...] = bits(first)
        filled = jnp.sum(first.astype(F32), axis=1, keepdims=True) > 0.5
        empty_scr[...] = jnp.where(filled | (iota((1, HEAD), 1) > 0), 0.0, EMPTY)

        seconds = (mine & is_second).astype(F32)
        there = jnp.sum(seconds, axis=1, keepdims=True) > 0.5
        code = jnp.where(there, jnp.sum(seconds * rank, axis=1, keepdims=True), NONE)
        short = jnp.max(second * (rank + 1.0), axis=1, keepdims=True) > EXTRA + 0.5
        place, lane = iota((CLUSTERS, HEAD), 0) % POOL, iota((CLUSTERS, HEAD), 1)
        codes = jnp.where(lane == place, code, 0.0)
        codes = jnp.where((lane == POOL) & short, 1.0, codes).astype(BF16)
        size = CLUSTERS // POOL * TAIL
        number = iota((size, CLUSTERS), 0)
        last = (number % TAIL == TAIL - 1) & (number // TAIL == iota((size, CLUSTERS), 1) // POOL)
        notes_scr[...] = dot(bits(last), codes)

        fits = is_second & (rank < EXTRA - 0.5)
        slot = jnp.where(fits, group * TAIL + rank, -1000.0)
        number = number.astype(F32)
        chosen_scr[...] = jnp.concatenate(
            [bits(number == slot + EXTRA * i) for i in range(3)], axis=1
        )

    data = [ref[...] for ref in (q_ref, k_ref, v_ref)]
    tail = dot(chosen_scr[...], jnp.concatenate(data, axis=0))
    tail = tail + jnp.concatenate([notes_scr[...]] * SHARE, axis=1)
    q, k, v = [dot(first_scr[...], one) for one in data]
    k = k + jnp.concatenate([empty_scr[...]] * SHARE, axis=1)
    for j in range(CLUSTERS // SHARE):
        rows = slice(j * SHARE, (j + 1) * SHARE)
        message = jnp.concatenate(
            [q[rows], k[rows], v[rows], tail[j * HALF : (j + 1) * HALF]], axis=0
        ).astype(BF16)
        for h in range(SHARE):
            place = (j // PAIR, h // CHIPS, j % PAIR, h % CHIPS)
            out_ref[place] = message[:, h * HEAD : (h + 1) * HEAD]


def lean_pack(row, queries, keys, values):
    data = pl.BlockSpec((TOK, SHARE * HEAD), lambda g: (0, g))
    shape = (CLUSTERS // POOL, HEADS // CHIPS, PAIR, CHIPS, MESSAGE, HEAD)
    block = shape[:1] + (SHARE // CHIPS,) + shape[2:]
    tails = CLUSTERS // POOL * TAIL
    return pl.pallas_call(
        lean_pack_kernel,
        grid=(GROUPS,),
        in_specs=[pl.BlockSpec((1, TOK), lambda g: (0, 0)), data, data, data],
        out_specs=pl.BlockSpec(block, lambda g: (0, g, 0, 0, 0, 0)),
        out_shape=jax.ShapeDtypeStruct(shape, BF16),
        scratch_shapes=[
            pltpu.VMEM((CLUSTERS, TOK), BF16),
            pltpu.VMEM((CLUSTERS, HEAD), F32),
            pltpu.VMEM((tails, HEAD), F32),
            pltpu.VMEM((tails, 3 * TOK), BF16),
        ],
        compiler_params=pltpu.CompilerParams(vmem_limit_bytes=VMEM),
        name="lean_pack",
    )(row, queries, keys, values)


def lean_attend_kernel(
    side_ref, in_ref, other_ref, out_ref, flag_ref, k_scr, v_scr, q_scr, o_scr, code_scr
):
    step = pl.program_id(0)
    side = side_ref[0]
    size = SHARE * CHUNK
    row, col = iota((size, size), 0), iota((size, size), 1)
    turn = bits(col == row % CHUNK * SHARE + row // CHUNK)
    turn_back = bits(row == col % CHUNK * SHARE + col // CHUNK)
    lane = iota((size, HEAD), 1)
    own_lane = lane == iota((size, HEAD), 0) // CHUNK + side * SHARE
    wide_row, wide_col = iota((size, CHUNK * TAIL), 0), iota((size, CHUNK * TAIL), 1)
    own_tail = wide_row % CHUNK == wide_col // TAIL
    wide_col = (wide_col + side * HALF) % TAIL
    pick_notes = bits(own_tail & (wide_col == TAIL - 1))
    tail_place = jnp.where(own_tail, wide_col.astype(F32), -200.0)
    back_place = jnp.where(row % CHUNK == col // SHARE, (col % SHARE).astype(F32), -200.0)

    def keep(part, start, q, k, v):
        shape = (SHARE, CHUNK, HEAD)
        q_scr[:, part : part + CHUNK, :] = q.astype(BF16).reshape(shape)
        v_scr[:, start : start + CHUNK, :] = v.astype(BF16).reshape(shape)
        k_scr[:, start : start + CHUNK, :HEAD] = k.astype(BF16).reshape(shape)
        mark = jnp.where(k > EMPTY / 2, MASKED, 0.0)
        k_scr[:, start : start + CHUNK, HEAD:] = mark.astype(BF16).reshape(shape)

    def load_all(here):
        flags = jnp.zeros((size, HEAD), F32)
        for block in range(SOURCES // CHUNK):
            part = in_ref[block * CHUNK : (block + 1) * CHUNK, :, :].astype(F32)
            pieces = [part[:, i * SHARE : (i + 1) * SHARE].reshape(size, HEAD) for i in range(3)]
            tall = jnp.concatenate(pieces, axis=1)
            mixed = dot(turn, tall.astype(BF16))
            start = here + block * CHUNK
            keep(block * CHUNK, start, mixed[:, :HEAD], mixed[:, HEAD : 2 * HEAD], mixed[:, 2 * HEAD :])

            other = other_ref[block * CHUNK : (block + 1) * CHUNK, :, :].astype(F32)
            tail = jnp.concatenate([part[:, 3 * SHARE :], other], axis=1)
            tail = tail.reshape(CHUNK * TAIL, HEAD).astype(BF16)
            notes = dot(pick_notes, tail)
            flags = jnp.maximum(flags, notes)
            code = jnp.sum(jnp.where(own_lane, notes, 0.0), axis=1, keepdims=True)
            code_scr[block] = jnp.broadcast_to(code, (size, HEAD))
            chosen = jnp.concatenate([bits(tail_place == code + EXTRA * i) for i in range(3)], axis=0)
            found = dot(chosen, tail)
            k = found[size : 2 * size] + jnp.where((code < NONE / 2) & (lane == 0), EMPTY, 0.0)
            start = here + SOURCES + block * CHUNK
            keep(SOURCES + block * CHUNK, start, found[:size], k, found[2 * size :])

        flags = jnp.max(flags, axis=0, keepdims=True)
        if here:
            flags = jnp.maximum(flags, flag_ref[0:1, :])
        flag_ref[...] = jnp.broadcast_to(flags, flag_ref.shape)

    def queries_of(block):
        start, stop = block * QBLK, (block + 1) * QBLK
        unit = bits(iota((QBLK, HEAD), 1) == 0)
        row, col = iota((QBLK, 1), 0), iota((1, QBLK), 1)
        row, col = [one % SOURCES * MOST + one // SOURCES for one in (row, col)]
        later = col > row
        ones = jnp.ones((stop, HEAD), BF16)
        for c in range(SHARE):
            q = jnp.concatenate([q_scr[c], unit], axis=1)
            v = jnp.concatenate([v_scr[c, 0:stop, :], ones], axis=1)
            scores = lax.dot_general(
                q, k_scr[c, 0:stop, :], (((1,), (1,)), ((), ())), preferred_element_type=F32
            )
            last = jnp.where(later, MASKED, scores[:, start:stop])
            if block:
                scores = jnp.concatenate([scores[:, :start], last], axis=1)
            else:
                scores = last
            top = jnp.max(scores, axis=1, keepdims=True)
            weights = jnp.exp2((scores - top) * FACTOR)
            mixed = dot(weights.astype(BF16), v)
            o_scr[c] = (mixed[:, :HEAD] / mixed[:, HEAD:]).astype(BF16)

    def store_all():
        for block in range(SOURCES // CHUNK):
            begin = block * CHUNK
            shape = (CHUNK, SHARE, HEAD)
            firsts = dot(turn_back, o_scr[:, begin : begin + CHUNK, :].reshape(size, HEAD))
            begin = begin + SOURCES
            chosen = bits(back_place == code_scr[block])
            seconds = lax.dot_general(
                chosen,
                o_scr[:, begin : begin + CHUNK, :].reshape(size, HEAD),
                (((0,), (0,)), ((), ())),
                preferred_element_type=F32,
            )
            both = jnp.concatenate([firsts.reshape(shape), seconds.reshape(shape)], axis=1)
            out_ref[block * CHUNK : (block + 1) * CHUNK, :, :] = both.astype(BF16)

    def work(number):
        load_all(number * QBLK)
        queries_of(number)
        store_all()

    for block in range(ROWS // QBLK):
        pl.when(step == block)(lambda block=block: work(block))


def lean_attend(side, received, other):
    part = pltpu.VMEM((SHARE, QBLK, HEAD), BF16)
    return pl.pallas_call(
        lean_attend_kernel,
        grid=(ROWS // QBLK,),
        in_specs=[
            pl.BlockSpec(memory_space=pltpu.SMEM),
            pl.BlockSpec((SOURCES, MESSAGE, HEAD), lambda b: (b, 0, 0)),
            pl.BlockSpec((SOURCES, HALF, HEAD), lambda b: (b, 0, 0)),
        ],
        out_specs=[
            pl.BlockSpec((SOURCES, UNIT, HEAD), lambda b: (b, 0, 0)),
            pl.BlockSpec((8, HEAD), lambda b: (0, 0)),
        ],
        out_shape=[
            jax.ShapeDtypeStruct((DEVICES, UNIT, HEAD), BF16),
            jax.ShapeDtypeStruct((8, HEAD), F32),
        ],
        scratch_shapes=[
            pltpu.VMEM((SHARE, ROWS, 2 * HEAD), BF16),
            pltpu.VMEM((SHARE, ROWS, HEAD), BF16),
            part,
            part,
            pltpu.VMEM((SOURCES // CHUNK, SHARE * CHUNK, HEAD), F32),
        ],
        compiler_params=pltpu.CompilerParams(vmem_limit_bytes=VMEM),
        name="lean_attend",
    )(side, received, other)


def lean_unpack_kernel(row_ref, in_ref, out_ref, onehot_scr):
    @pl.when(pl.program_id(0) == 0)
    def prepare():
        row, _, second, rank = token_ranks(row_ref[...])
        owner = jnp.floor(row / SHARE)
        slot = owner * UNIT + jnp.where(second > 0.5, SHARE + rank, row - owner * SHARE)
        onehot_scr[...] = bits(iota(onehot_scr.shape, 0).astype(F32) == slot)

    rows = jnp.concatenate(
        [
            jnp.concatenate(
                [in_ref[j // PAIR, h // CHIPS, j % PAIR, h % CHIPS] for h in range(SHARE)], axis=1
            )
            for j in range(CLUSTERS // SHARE)
        ],
        axis=0,
    )
    out_ref[...] = lax.dot_general(
        onehot_scr[...], rows, (((0,), (0,)), ((), ())), preferred_element_type=F32
    ).astype(BF16)


def lean_unpack(row, back):
    block = (CLUSTERS // POOL, SHARE // CHIPS, PAIR, CHIPS, UNIT, HEAD)
    return pl.pallas_call(
        lean_unpack_kernel,
        grid=(GROUPS,),
        in_specs=[
            pl.BlockSpec((1, TOK), lambda g: (0, 0)),
            pl.BlockSpec(block, lambda g: (0, g, 0, 0, 0, 0)),
        ],
        out_specs=pl.BlockSpec((TOK, SHARE * HEAD), lambda g: (0, g)),
        out_shape=jax.ShapeDtypeStruct((TOK, HEADS * HEAD), BF16),
        scratch_shapes=[pltpu.VMEM((CLUSTERS // SHARE * UNIT, TOK), BF16)],
        compiler_params=pltpu.CompilerParams(vmem_limit_bytes=63 * 1024 * 1024),
        name="lean_unpack",
    )(row, back)


def exchange(data):
    return lax.all_to_all(data, ("seq", "blk"), split_axis=0, concat_axis=0, tiled=True)


def body(queries, keys, values, cluster_ids):
    row = cluster_ids.reshape(1, TOK)
    sent = lean_pack(row, queries, keys, values)
    received = exchange(sent.reshape(DEVICES, MESSAGE, HEAD))
    swap = [(i, i ^ 1) for i in range(CLUSTERS)]
    other = lax.ppermute(received[:, 3 * SHARE :, :], "seq", swap)
    side = (lax.axis_index("seq") % PAIR).astype(jnp.int32).reshape(1)
    mixed, flags = lean_attend(side, received, other)
    back = exchange(mixed)
    short = flags[0, POOL] > 0.5

    def lean(back, row, queries, keys, values):
        back = back.reshape(CLUSTERS // POOL, HEADS // CHIPS, PAIR, CHIPS, UNIT, HEAD)
        return lean_unpack(row, back)

    def full(back, row, queries, keys, values):
        sent = pack(row, queries, keys, values)
        back = exchange(attend(exchange(sent.reshape(DEVICES, 3 * UNIT, HEAD))))
        return unpack(row, back.reshape(CLUSTERS, GROUPS, UNIT, HEAD))

    return lax.cond(short, full, lean, back, row, queries, keys, values)


def solution(mesh):
    spec = P(("seq", "blk"), None)
    return jax.shard_map(
        body, mesh=mesh, in_specs=(spec,) * 4, out_specs=spec, check_vma=False
    )
```

```python
import jax
import jax.numpy as jnp
from jax import lax
from jax.experimental import pallas as pl
from jax.experimental.pallas import tpu as pltpu
from jax.sharding import PartitionSpec as P

HEADS = 32
HEAD = 128
TOK = 128
CLUSTERS = 128
MOST = 2
GROUPS = 4
SHARE = HEADS // GROUPS
UNIT = SHARE * MOST
DEVICES = CLUSTERS * GROUPS
ROWS = DEVICES * MOST
QBLK = 256
SOURCES = QBLK // MOST
CHUNK = 16
VMEM = 56 * 1024 * 1024
PAIR = 2
POOL = PAIR * SHARE
EXTRA = 5
TAIL = 16
HALF = TAIL // PAIR
MESSAGE = 3 * SHARE + HALF
CHIPS = 4
WIDE = 16
NONE = -64.0
EMPTY = 256.0
MASKED = -1e30
FACTOR = 1.4426950408889634 / HEAD**0.5
BF16 = jnp.bfloat16
F32 = jnp.float32


def iota(shape, dim):
    return lax.broadcasted_iota(jnp.int32, shape, dim)


def spread_matrix(inverse):
    size = CHUNK * UNIT
    out, src = iota((size, size), 0), iota((size, size), 1)
    if inverse:
        out, src = src, out
    h, d, s = out // (CHUNK * MOST), (out // MOST) % CHUNK, out % MOST
    return (src == d * UNIT + h * MOST + s).astype(F32).astype(BF16)


def slot_onehot(row):
    row = row.astype(F32)
    above, across = iota((TOK, TOK), 0), iota((TOK, TOK), 1)
    col = jnp.sum(jnp.where(above == across, row, 0.0), axis=1, keepdims=True)
    earlier = (col == row) & (above < across)
    slots = row * MOST + jnp.sum(earlier.astype(F32), axis=0, keepdims=True)
    return (iota((CLUSTERS * MOST, TOK), 0).astype(F32) == slots).astype(F32)


def dot(a, b):
    return jnp.dot(a, b, preferred_element_type=F32)


def pack_kernel(row_ref, q_ref, k_ref, v_ref, out_ref):
    onehot = slot_onehot(row_ref[...])
    filled = jnp.sum(onehot, axis=1, keepdims=True) > 0.5
    onehot = onehot.astype(BF16)
    empty_entry = jnp.where(filled | (iota((1, HEAD), 1) > 0), 0.0, EMPTY)
    empty_entry = jnp.concatenate([empty_entry] * SHARE, axis=1)
    scatter = spread_matrix(True)
    rows = [dot(onehot, ref[...]) for ref in (q_ref, k_ref, v_ref)]
    rows[1] = rows[1] + empty_entry
    rows = [one.astype(BF16) for one in rows]
    width = CHUNK * MOST
    for block in range(CLUSTERS // CHUNK):
        tall = jnp.concatenate(
            [
                jnp.concatenate(
                    [
                        one[block * width : (block + 1) * width, h * HEAD : (h + 1) * HEAD]
                        for h in range(SHARE)
                    ],
                    axis=0,
                )
                for one in rows
            ],
            axis=1,
        )
        mixed = dot(scatter, tall).astype(BF16)
        for index in range(3):
            out_ref[
                block * CHUNK : (block + 1) * CHUNK, 0, index * UNIT : (index + 1) * UNIT, :
            ] = mixed[:, index * HEAD : (index + 1) * HEAD].reshape(CHUNK, UNIT, HEAD)


def pack(row, queries, keys, values):
    data = pl.BlockSpec((TOK, SHARE * HEAD), lambda g: (0, g))
    return pl.pallas_call(
        pack_kernel,
        grid=(GROUPS,),
        in_specs=[pl.BlockSpec((1, TOK), lambda g: (0, 0)), data, data, data],
        out_specs=pl.BlockSpec((CLUSTERS, 1, 3 * UNIT, HEAD), lambda g: (0, g, 0, 0)),
        out_shape=jax.ShapeDtypeStruct((CLUSTERS, GROUPS, 3 * UNIT, HEAD), BF16),
        compiler_params=pltpu.CompilerParams(vmem_limit_bytes=VMEM),
        name="pack",
    )(row, queries, keys, values)


def attend_kernel(in_ref, out_ref, k_scr, v_scr, q_scr, o_scr, mark_scr):
    step = pl.program_id(0)
    gather, scatter = spread_matrix(False), spread_matrix(True)
    first_lane = iota((QBLK, HEAD), 1) == 0

    def regroup(block):
        part = in_ref[block * CHUNK : (block + 1) * CHUNK, :, :]
        tall = jnp.concatenate(
            [
                part[:, i * UNIT : (i + 1) * UNIT, :].reshape(CHUNK * UNIT, HEAD)
                for i in range(3)
            ],
            axis=1,
        )
        mixed = dot(gather, tall).astype(BF16)
        width = CHUNK * MOST
        start = pl.multiple_of(step * QBLK + block * width, width)
        q_scr[:, block * width : (block + 1) * width, :] = mixed[:, :HEAD].reshape(
            SHARE, width, HEAD
        )
        k_scr[:, pl.ds(start, width), :] = mixed[:, HEAD : 2 * HEAD].reshape(SHARE, width, HEAD)
        v_scr[:, pl.ds(start, width), :] = mixed[:, 2 * HEAD :].reshape(SHARE, width, HEAD)

    for block in range(SOURCES // CHUNK):
        regroup(block)

    here = pl.multiple_of(step * QBLK, QBLK)
    empty = k_scr[0, pl.ds(here, QBLK), :].astype(F32) > EMPTY / 2
    mark_scr[pl.ds(here, QBLK), :] = jnp.where(empty & first_lane, MASKED, 0.0).astype(BF16)

    def queries_of(block):
        start, stop = block * QBLK, (block + 1) * QBLK
        unit = first_lane.astype(F32).astype(BF16)
        later = iota((QBLK, QBLK), 1) > iota((QBLK, QBLK), 0)
        ones = jnp.ones((stop, HEAD), BF16)
        for h in range(SHARE):
            q = jnp.concatenate([q_scr[h], unit], axis=1)
            k = jnp.concatenate([k_scr[h, 0:stop, :], mark_scr[0:stop, :]], axis=1)
            v = jnp.concatenate([v_scr[h, 0:stop, :], ones], axis=1)
            scores = lax.dot_general(
                q, k, (((1,), (1,)), ((), ())), preferred_element_type=F32
            )
            last = jnp.where(later, MASKED, scores[:, start:stop])
            if block:
                scores = jnp.concatenate([scores[:, :start], last], axis=1)
            else:
                scores = last
            top = jnp.max(scores, axis=1, keepdims=True)
            weights = jnp.exp2((scores - top) * FACTOR)
            mixed = dot(weights.astype(BF16), v)
            o_scr[h] = (mixed[:, :HEAD] / mixed[:, HEAD:]).astype(BF16)

    for block in range(ROWS // QBLK):
        pl.when(step == block)(lambda block=block: queries_of(block))

    for block in range(SOURCES // CHUNK):
        width = CHUNK * MOST
        tall = o_scr[:, block * width : (block + 1) * width, :].reshape(CHUNK * UNIT, HEAD)
        mixed = dot(scatter, tall).astype(BF16)
        out_ref[block * CHUNK : (block + 1) * CHUNK, :, :] = mixed.reshape(CHUNK, UNIT, HEAD)


def attend(received):
    held = pltpu.VMEM((SHARE, ROWS, HEAD), BF16)
    part = pltpu.VMEM((SHARE, QBLK, HEAD), BF16)
    return pl.pallas_call(
        attend_kernel,
        grid=(ROWS // QBLK,),
        in_specs=[pl.BlockSpec((SOURCES, 3 * UNIT, HEAD), lambda b: (b, 0, 0))],
        out_specs=pl.BlockSpec((SOURCES, UNIT, HEAD), lambda b: (b, 0, 0)),
        out_shape=jax.ShapeDtypeStruct((DEVICES, UNIT, HEAD), BF16),
        scratch_shapes=[held, held, part, part, pltpu.VMEM((ROWS, HEAD), BF16)],
        compiler_params=pltpu.CompilerParams(vmem_limit_bytes=VMEM),
        name="attend",
    )(received)


def unpack_kernel(row_ref, in_ref, out_ref):
    onehot = slot_onehot(row_ref[...]).astype(BF16)
    gather = spread_matrix(False)
    width = CHUNK * MOST
    blocks = []
    for block in range(CLUSTERS // CHUNK):
        tall = in_ref[block * CHUNK : (block + 1) * CHUNK, 0, :, :].reshape(CHUNK * UNIT, HEAD)
        mixed = dot(gather, tall).astype(BF16)
        blocks.append(
            jnp.concatenate([mixed[h * width : (h + 1) * width, :] for h in range(SHARE)], axis=1)
        )
    rows = jnp.concatenate(blocks, axis=0)
    out_ref[...] = lax.dot_general(
        onehot, rows, (((0,), (0,)), ((), ())), preferred_element_type=F32
    ).astype(BF16)


def unpack(row, back):
    return pl.pallas_call(
        unpack_kernel,
        grid=(GROUPS,),
        in_specs=[
            pl.BlockSpec((1, TOK), lambda g: (0, 0)),
            pl.BlockSpec((CLUSTERS, 1, UNIT, HEAD), lambda g: (0, g, 0, 0)),
        ],
        out_specs=pl.BlockSpec((TOK, SHARE * HEAD), lambda g: (0, g)),
        out_shape=jax.ShapeDtypeStruct((TOK, HEADS * HEAD), BF16),
        compiler_params=pltpu.CompilerParams(vmem_limit_bytes=VMEM),
        name="unpack",
    )(row, back)


def token_ranks(row):
    row = row.astype(F32)
    above, across = iota((TOK, TOK), 0), iota((TOK, TOK), 1)
    col = jnp.sum(jnp.where(above == across, row, 0.0), axis=1, keepdims=True)
    same = col == row
    second = jnp.sum((same & (above < across)).astype(F32), axis=0, keepdims=True)
    second_col = jnp.sum((same & (across < above)).astype(F32), axis=1, keepdims=True)
    group, group_col = jnp.floor(row / POOL), jnp.floor(col / POOL)
    lower = (second_col > 0.5) & (group_col == group) & (col < row)
    rank = jnp.sum(lower.astype(F32), axis=0, keepdims=True)
    return row, group, second, rank


def bits(mask):
    return mask.astype(F32).astype(BF16)


def lean_pack_kernel(
    row_ref, q_ref, k_ref, v_ref, out_ref, first_scr, empty_scr, notes_scr, chosen_scr
):
    @pl.when(pl.program_id(0) == 0)
    def prepare():
        row, group, second, rank = token_ranks(row_ref[...])
        is_second = second > 0.5
        mine = iota((CLUSTERS, TOK), 0).astype(F32) == row
        first = mine & jnp.logical_not(is_second)
        first_scr[...] = bits(first)
        filled = jnp.sum(first.astype(F32), axis=1, keepdims=True) > 0.5
        empty_scr[...] = jnp.where(filled | (iota((1, HEAD), 1) > 0), 0.0, EMPTY)

        seconds = (mine & is_second).astype(F32)
        there = jnp.sum(seconds, axis=1, keepdims=True) > 0.5
        code = jnp.where(there, jnp.sum(seconds * rank, axis=1, keepdims=True), NONE)
        short = jnp.max(second * (rank + 1.0), axis=1, keepdims=True) > EXTRA + 0.5
        place, lane = iota((CLUSTERS, HEAD), 0) % POOL, iota((CLUSTERS, HEAD), 1)
        codes = jnp.where(lane == place, code, 0.0)
        codes = jnp.where((lane == POOL) & short, 1.0, codes).astype(BF16)
        size = CLUSTERS // POOL * TAIL
        number = iota((size, CLUSTERS), 0)
        last = (number % TAIL == TAIL - 1) & (number // TAIL == iota((size, CLUSTERS), 1) // POOL)
        notes_scr[...] = dot(bits(last), codes)

        fits = is_second & (rank < EXTRA - 0.5)
        slot = jnp.where(fits, group * TAIL + rank, -1000.0)
        number = number.astype(F32)
        chosen_scr[...] = jnp.concatenate(
            [bits(number == slot + EXTRA * i) for i in range(3)], axis=1
        )

    data = [ref[...] for ref in (q_ref, k_ref, v_ref)]
    tail = dot(chosen_scr[...], jnp.concatenate(data, axis=0))
    tail = tail + jnp.concatenate([notes_scr[...]] * WIDE, axis=1)
    q, k, v = [dot(first_scr[...], one) for one in data]
    k = k + jnp.concatenate([empty_scr[...]] * WIDE, axis=1)
    for j in range(CLUSTERS // SHARE):
        rows = slice(j * SHARE, (j + 1) * SHARE)
        message = jnp.concatenate(
            [q[rows], k[rows], v[rows], tail[j * HALF : (j + 1) * HALF]], axis=0
        ).astype(BF16)
        for h in range(WIDE):
            place = (j // PAIR, h // CHIPS, j % PAIR, h % CHIPS)
            out_ref[place] = message[:, h * HEAD : (h + 1) * HEAD]


def lean_pack(row, queries, keys, values):
    data = pl.BlockSpec((TOK, WIDE * HEAD), lambda g: (0, g))
    shape = (CLUSTERS // POOL, HEADS // CHIPS, PAIR, CHIPS, MESSAGE, HEAD)
    block = shape[:1] + (WIDE // CHIPS,) + shape[2:]
    tails = CLUSTERS // POOL * TAIL
    return pl.pallas_call(
        lean_pack_kernel,
        grid=(HEADS // WIDE,),
        in_specs=[pl.BlockSpec((1, TOK), lambda g: (0, 0)), data, data, data],
        out_specs=pl.BlockSpec(block, lambda g: (0, g, 0, 0, 0, 0)),
        out_shape=jax.ShapeDtypeStruct(shape, BF16),
        scratch_shapes=[
            pltpu.VMEM((CLUSTERS, TOK), BF16),
            pltpu.VMEM((CLUSTERS, HEAD), F32),
            pltpu.VMEM((tails, HEAD), F32),
            pltpu.VMEM((tails, 3 * TOK), BF16),
        ],
        compiler_params=pltpu.CompilerParams(vmem_limit_bytes=VMEM),
        name="lean_pack",
    )(row, queries, keys, values)


def lean_attend_kernel(
    side_ref, in_ref, other_ref, out_ref, flag_ref, k_scr, v_scr, q_scr, o_scr, code_scr
):
    step = pl.program_id(0)
    side = side_ref[0]
    size = SHARE * CHUNK
    row, col = iota((size, size), 0), iota((size, size), 1)
    turn = bits(col == row % CHUNK * SHARE + row // CHUNK)
    turn_back = bits(row == col % CHUNK * SHARE + col // CHUNK)
    lane = iota((size, HEAD), 1)
    own_lane = lane == iota((size, HEAD), 0) // CHUNK + side * SHARE
    wide_row, wide_col = iota((size, CHUNK * TAIL), 0), iota((size, CHUNK * TAIL), 1)
    own_tail = wide_row % CHUNK == wide_col // TAIL
    wide_col = (wide_col + side * HALF) % TAIL
    pick_notes = bits(own_tail & (wide_col == TAIL - 1))
    tail_place = jnp.where(own_tail, wide_col.astype(F32), -200.0)
    back_place = jnp.where(row % CHUNK == col // SHARE, (col % SHARE).astype(F32), -200.0)

    def keep(part, start, q, k, v):
        shape = (SHARE, CHUNK, HEAD)
        q_scr[:, part : part + CHUNK, :] = q.astype(BF16).reshape(shape)
        v_scr[:, start : start + CHUNK, :] = v.astype(BF16).reshape(shape)
        k_scr[:, start : start + CHUNK, :HEAD] = k.astype(BF16).reshape(shape)
        mark = jnp.where(k > EMPTY / 2, MASKED, 0.0)
        k_scr[:, start : start + CHUNK, HEAD:] = mark.astype(BF16).reshape(shape)

    def load_all(here):
        flags = jnp.zeros((size, HEAD), F32)
        for block in range(SOURCES // CHUNK):
            part = in_ref[block * CHUNK : (block + 1) * CHUNK, :, :].astype(F32)
            pieces = [part[:, i * SHARE : (i + 1) * SHARE].reshape(size, HEAD) for i in range(3)]
            tall = jnp.concatenate(pieces, axis=1)
            mixed = dot(turn, tall.astype(BF16))
            start = here + block * CHUNK
            keep(block * CHUNK, start, mixed[:, :HEAD], mixed[:, HEAD : 2 * HEAD], mixed[:, 2 * HEAD :])

            other = other_ref[block * CHUNK : (block + 1) * CHUNK, :, :].astype(F32)
            tail = jnp.concatenate([part[:, 3 * SHARE :], other], axis=1)
            tail = tail.reshape(CHUNK * TAIL, HEAD).astype(BF16)
            notes = dot(pick_notes, tail)
            flags = jnp.maximum(flags, notes)
            code = jnp.sum(jnp.where(own_lane, notes, 0.0), axis=1, keepdims=True)
            code_scr[block] = jnp.broadcast_to(code, (size, HEAD))
            chosen = jnp.concatenate([bits(tail_place == code + EXTRA * i) for i in range(3)], axis=0)
            found = dot(chosen, tail)
            k = found[size : 2 * size] + jnp.where((code < NONE / 2) & (lane == 0), EMPTY, 0.0)
            start = here + SOURCES + block * CHUNK
            keep(SOURCES + block * CHUNK, start, found[:size], k, found[2 * size :])

        flags = jnp.max(flags, axis=0, keepdims=True)
        if here:
            flags = jnp.maximum(flags, flag_ref[0:1, :])
        flag_ref[...] = jnp.broadcast_to(flags, flag_ref.shape)

    def queries_of(block):
        start, stop = block * QBLK, (block + 1) * QBLK
        unit = bits(iota((QBLK, HEAD), 1) == 0)
        row, col = iota((QBLK, 1), 0), iota((1, QBLK), 1)
        row, col = [one % SOURCES * MOST + one // SOURCES for one in (row, col)]
        later = col > row
        ones = jnp.ones((stop, HEAD), BF16)
        for c in range(SHARE):
            q = jnp.concatenate([q_scr[c], unit], axis=1)
            v = jnp.concatenate([v_scr[c, 0:stop, :], ones], axis=1)
            scores = lax.dot_general(
                q, k_scr[c, 0:stop, :], (((1,), (1,)), ((), ())), preferred_element_type=F32
            )
            last = jnp.where(later, MASKED, scores[:, start:stop])
            if block:
                scores = jnp.concatenate([scores[:, :start], last], axis=1)
            else:
                scores = last
            top = jnp.max(scores, axis=1, keepdims=True)
            weights = jnp.exp2((scores - top) * FACTOR)
            mixed = dot(weights.astype(BF16), v)
            o_scr[c] = (mixed[:, :HEAD] / mixed[:, HEAD:]).astype(BF16)

    def store_all():
        for block in range(SOURCES // CHUNK):
            begin = block * CHUNK
            shape = (CHUNK, SHARE, HEAD)
            firsts = dot(turn_back, o_scr[:, begin : begin + CHUNK, :].reshape(size, HEAD))
            begin = begin + SOURCES
            chosen = bits(back_place == code_scr[block])
            seconds = lax.dot_general(
                chosen,
                o_scr[:, begin : begin + CHUNK, :].reshape(size, HEAD),
                (((0,), (0,)), ((), ())),
                preferred_element_type=F32,
            )
            both = jnp.concatenate([firsts.reshape(shape), seconds.reshape(shape)], axis=1)
            out_ref[block * CHUNK : (block + 1) * CHUNK, :, :] = both.astype(BF16)

    def work(number):
        load_all(number * QBLK)
        queries_of(number)
        store_all()

    for block in range(ROWS // QBLK):
        pl.when(step == block)(lambda block=block: work(block))


def lean_attend(side, received, other):
    part = pltpu.VMEM((SHARE, QBLK, HEAD), BF16)
    return pl.pallas_call(
        lean_attend_kernel,
        grid=(ROWS // QBLK,),
        in_specs=[
            pl.BlockSpec(memory_space=pltpu.SMEM),
            pl.BlockSpec((SOURCES, MESSAGE, HEAD), lambda b: (b, 0, 0)),
            pl.BlockSpec((SOURCES, HALF, HEAD), lambda b: (b, 0, 0)),
        ],
        out_specs=[
            pl.BlockSpec((SOURCES, UNIT, HEAD), lambda b: (b, 0, 0)),
            pl.BlockSpec((8, HEAD), lambda b: (0, 0)),
        ],
        out_shape=[
            jax.ShapeDtypeStruct((DEVICES, UNIT, HEAD), BF16),
            jax.ShapeDtypeStruct((8, HEAD), F32),
        ],
        scratch_shapes=[
            pltpu.VMEM((SHARE, ROWS, 2 * HEAD), BF16),
            pltpu.VMEM((SHARE, ROWS, HEAD), BF16),
            part,
            part,
            pltpu.VMEM((SOURCES // CHUNK, SHARE * CHUNK, HEAD), F32),
        ],
        compiler_params=pltpu.CompilerParams(vmem_limit_bytes=VMEM // 2),
        name="lean_attend",
    )(side, received, other)


def lean_unpack_kernel(row_ref, in_ref, out_ref, onehot_scr):
    @pl.when(pl.program_id(0) == 0)
    def prepare():
        row, _, second, rank = token_ranks(row_ref[...])
        owner = jnp.floor(row / SHARE)
        slot = owner * UNIT + jnp.where(second > 0.5, SHARE + rank, row - owner * SHARE)
        onehot_scr[...] = bits(iota(onehot_scr.shape, 0).astype(F32) == slot)

    rows = jnp.concatenate(
        [
            jnp.concatenate(
                [in_ref[j // PAIR, h // CHIPS, j % PAIR, h % CHIPS] for h in range(WIDE)], axis=1
            )
            for j in range(CLUSTERS // SHARE)
        ],
        axis=0,
    )
    out_ref[...] = lax.dot_general(
        onehot_scr[...], rows, (((0,), (0,)), ((), ())), preferred_element_type=F32
    ).astype(BF16)


def lean_unpack(row, back):
    block = (CLUSTERS // POOL, WIDE // CHIPS, PAIR, CHIPS, UNIT, HEAD)
    return pl.pallas_call(
        lean_unpack_kernel,
        grid=(HEADS // WIDE,),
        in_specs=[
            pl.BlockSpec((1, TOK), lambda g: (0, 0)),
            pl.BlockSpec(block, lambda g: (0, g, 0, 0, 0, 0)),
        ],
        out_specs=pl.BlockSpec((TOK, WIDE * HEAD), lambda g: (0, g)),
        out_shape=jax.ShapeDtypeStruct((TOK, HEADS * HEAD), BF16),
        scratch_shapes=[pltpu.VMEM((CLUSTERS // SHARE * UNIT, TOK), BF16)],
        compiler_params=pltpu.CompilerParams(vmem_limit_bytes=63 * 1024 * 1024),
        name="lean_unpack",
    )(row, back)


def exchange(data):
    return lax.all_to_all(data, ("seq", "blk"), split_axis=0, concat_axis=0, tiled=True)


def body(queries, keys, values, cluster_ids):
    row = cluster_ids.reshape(1, TOK)
    sent = lean_pack(row, queries, keys, values)
    received = exchange(sent.reshape(DEVICES, MESSAGE, HEAD))
    swap = [(i, i ^ 1) for i in range(CLUSTERS)]
    other = lax.ppermute(received[:, 3 * SHARE :, :], "seq", swap)
    side = (lax.axis_index("seq") % PAIR).astype(jnp.int32).reshape(1)
    mixed, flags = lean_attend(side, received, other)
    back = exchange(mixed)
    short = flags[0, POOL] > 0.5

    def lean(back, row, queries, keys, values):
        back = back.reshape(CLUSTERS // POOL, HEADS // CHIPS, PAIR, CHIPS, UNIT, HEAD)
        return lean_unpack(row, back)

    def full(back, row, queries, keys, values):
        sent = pack(row, queries, keys, values)
        back = exchange(attend(exchange(sent.reshape(DEVICES, 3 * UNIT, HEAD))))
        return unpack(row, back.reshape(CLUSTERS, GROUPS, UNIT, HEAD))

    return lax.cond(short, full, lean, back, row, queries, keys, values)


def solution(mesh):
    spec = P(("seq", "blk"), None)
    return jax.shard_map(
        body, mesh=mesh, in_specs=(spec,) * 4, out_specs=spec, check_vma=False
    )
```

```python
import jax
import jax.numpy as jnp
from jax import lax
from jax.experimental import pallas as pl
from jax.experimental.pallas import tpu as pltpu
from jax.sharding import PartitionSpec as P

HEADS = 32
HEAD = 128
TOK = 128
CLUSTERS = 128
MOST = 2
GROUPS = 4
SHARE = HEADS // GROUPS
UNIT = SHARE * MOST
DEVICES = CLUSTERS * GROUPS
ROWS = DEVICES * MOST
QBLK = 256
SOURCES = QBLK // MOST
CHUNK = 16
VMEM = 56 * 1024 * 1024
ALL_VMEM = 63 * 1024 * 1024
PAIR = 2
POOL = PAIR * SHARE
EXTRA = 5
TAIL = 16
HALF = TAIL // PAIR
MESSAGE = 3 * SHARE + HALF
CHIPS = 4
WIDE = 16
NONE = -64.0
EMPTY = 256.0
MASKED = -1e30
FACTOR = 1.4426950408889634 / HEAD**0.5
BF16 = jnp.bfloat16
F32 = jnp.float32


def iota(shape, dim):
    return lax.broadcasted_iota(jnp.int32, shape, dim)


def spread_matrix(inverse):
    size = CHUNK * UNIT
    out, src = iota((size, size), 0), iota((size, size), 1)
    if inverse:
        out, src = src, out
    h, d, s = out // (CHUNK * MOST), (out // MOST) % CHUNK, out % MOST
    return (src == d * UNIT + h * MOST + s).astype(F32).astype(BF16)


def slot_onehot(row):
    row = row.astype(F32)
    above, across = iota((TOK, TOK), 0), iota((TOK, TOK), 1)
    col = jnp.sum(jnp.where(above == across, row, 0.0), axis=1, keepdims=True)
    earlier = (col == row) & (above < across)
    slots = row * MOST + jnp.sum(earlier.astype(F32), axis=0, keepdims=True)
    return (iota((CLUSTERS * MOST, TOK), 0).astype(F32) == slots).astype(F32)


def dot(a, b):
    return jnp.dot(a, b, preferred_element_type=F32)


def pack_kernel(row_ref, q_ref, k_ref, v_ref, out_ref):
    onehot = slot_onehot(row_ref[...])
    filled = jnp.sum(onehot, axis=1, keepdims=True) > 0.5
    onehot = onehot.astype(BF16)
    empty_entry = jnp.where(filled | (iota((1, HEAD), 1) > 0), 0.0, EMPTY)
    empty_entry = jnp.concatenate([empty_entry] * SHARE, axis=1)
    scatter = spread_matrix(True)
    rows = [dot(onehot, ref[...]) for ref in (q_ref, k_ref, v_ref)]
    rows[1] = rows[1] + empty_entry
    rows = [one.astype(BF16) for one in rows]
    width = CHUNK * MOST
    for block in range(CLUSTERS // CHUNK):
        tall = jnp.concatenate(
            [
                jnp.concatenate(
                    [
                        one[block * width : (block + 1) * width, h * HEAD : (h + 1) * HEAD]
                        for h in range(SHARE)
                    ],
                    axis=0,
                )
                for one in rows
            ],
            axis=1,
        )
        mixed = dot(scatter, tall).astype(BF16)
        for index in range(3):
            out_ref[
                block * CHUNK : (block + 1) * CHUNK, 0, index * UNIT : (index + 1) * UNIT, :
            ] = mixed[:, index * HEAD : (index + 1) * HEAD].reshape(CHUNK, UNIT, HEAD)


def pack(row, queries, keys, values):
    data = pl.BlockSpec((TOK, SHARE * HEAD), lambda g: (0, g))
    return pl.pallas_call(
        pack_kernel,
        grid=(GROUPS,),
        in_specs=[pl.BlockSpec((1, TOK), lambda g: (0, 0)), data, data, data],
        out_specs=pl.BlockSpec((CLUSTERS, 1, 3 * UNIT, HEAD), lambda g: (0, g, 0, 0)),
        out_shape=jax.ShapeDtypeStruct((CLUSTERS, GROUPS, 3 * UNIT, HEAD), BF16),
        compiler_params=pltpu.CompilerParams(vmem_limit_bytes=VMEM),
        name="pack",
    )(row, queries, keys, values)


def attend_kernel(in_ref, out_ref, k_scr, v_scr, q_scr, o_scr, mark_scr):
    step = pl.program_id(0)
    gather, scatter = spread_matrix(False), spread_matrix(True)
    first_lane = iota((QBLK, HEAD), 1) == 0

    def regroup(block):
        part = in_ref[block * CHUNK : (block + 1) * CHUNK, :, :]
        tall = jnp.concatenate(
            [
                part[:, i * UNIT : (i + 1) * UNIT, :].reshape(CHUNK * UNIT, HEAD)
                for i in range(3)
            ],
            axis=1,
        )
        mixed = dot(gather, tall).astype(BF16)
        width = CHUNK * MOST
        start = pl.multiple_of(step * QBLK + block * width, width)
        q_scr[:, block * width : (block + 1) * width, :] = mixed[:, :HEAD].reshape(
            SHARE, width, HEAD
        )
        k_scr[:, pl.ds(start, width), :] = mixed[:, HEAD : 2 * HEAD].reshape(SHARE, width, HEAD)
        v_scr[:, pl.ds(start, width), :] = mixed[:, 2 * HEAD :].reshape(SHARE, width, HEAD)

    for block in range(SOURCES // CHUNK):
        regroup(block)

    here = pl.multiple_of(step * QBLK, QBLK)
    empty = k_scr[0, pl.ds(here, QBLK), :].astype(F32) > EMPTY / 2
    mark_scr[pl.ds(here, QBLK), :] = jnp.where(empty & first_lane, MASKED, 0.0).astype(BF16)

    def queries_of(block):
        start, stop = block * QBLK, (block + 1) * QBLK
        unit = first_lane.astype(F32).astype(BF16)
        later = iota((QBLK, QBLK), 1) > iota((QBLK, QBLK), 0)
        ones = jnp.ones((stop, HEAD), BF16)
        for h in range(SHARE):
            q = jnp.concatenate([q_scr[h], unit], axis=1)
            k = jnp.concatenate([k_scr[h, 0:stop, :], mark_scr[0:stop, :]], axis=1)
            v = jnp.concatenate([v_scr[h, 0:stop, :], ones], axis=1)
            scores = lax.dot_general(
                q, k, (((1,), (1,)), ((), ())), preferred_element_type=F32
            )
            last = jnp.where(later, MASKED, scores[:, start:stop])
            if block:
                scores = jnp.concatenate([scores[:, :start], last], axis=1)
            else:
                scores = last
            top = jnp.max(scores, axis=1, keepdims=True)
            weights = jnp.exp2((scores - top) * FACTOR)
            mixed = dot(weights.astype(BF16), v)
            o_scr[h] = (mixed[:, :HEAD] / mixed[:, HEAD:]).astype(BF16)

    for block in range(ROWS // QBLK):
        pl.when(step == block)(lambda block=block: queries_of(block))

    for block in range(SOURCES // CHUNK):
        width = CHUNK * MOST
        tall = o_scr[:, block * width : (block + 1) * width, :].reshape(CHUNK * UNIT, HEAD)
        mixed = dot(scatter, tall).astype(BF16)
        out_ref[block * CHUNK : (block + 1) * CHUNK, :, :] = mixed.reshape(CHUNK, UNIT, HEAD)


def attend(received):
    held = pltpu.VMEM((SHARE, ROWS, HEAD), BF16)
    part = pltpu.VMEM((SHARE, QBLK, HEAD), BF16)
    return pl.pallas_call(
        attend_kernel,
        grid=(ROWS // QBLK,),
        in_specs=[pl.BlockSpec((SOURCES, 3 * UNIT, HEAD), lambda b: (b, 0, 0))],
        out_specs=pl.BlockSpec((SOURCES, UNIT, HEAD), lambda b: (b, 0, 0)),
        out_shape=jax.ShapeDtypeStruct((DEVICES, UNIT, HEAD), BF16),
        scratch_shapes=[held, held, part, part, pltpu.VMEM((ROWS, HEAD), BF16)],
        compiler_params=pltpu.CompilerParams(vmem_limit_bytes=VMEM),
        name="attend",
    )(received)


def unpack_kernel(row_ref, in_ref, out_ref):
    onehot = slot_onehot(row_ref[...]).astype(BF16)
    gather = spread_matrix(False)
    width = CHUNK * MOST
    blocks = []
    for block in range(CLUSTERS // CHUNK):
        tall = in_ref[block * CHUNK : (block + 1) * CHUNK, 0, :, :].reshape(CHUNK * UNIT, HEAD)
        mixed = dot(gather, tall).astype(BF16)
        blocks.append(
            jnp.concatenate([mixed[h * width : (h + 1) * width, :] for h in range(SHARE)], axis=1)
        )
    rows = jnp.concatenate(blocks, axis=0)
    out_ref[...] = lax.dot_general(
        onehot, rows, (((0,), (0,)), ((), ())), preferred_element_type=F32
    ).astype(BF16)


def unpack(row, back):
    return pl.pallas_call(
        unpack_kernel,
        grid=(GROUPS,),
        in_specs=[
            pl.BlockSpec((1, TOK), lambda g: (0, 0)),
            pl.BlockSpec((CLUSTERS, 1, UNIT, HEAD), lambda g: (0, g, 0, 0)),
        ],
        out_specs=pl.BlockSpec((TOK, SHARE * HEAD), lambda g: (0, g)),
        out_shape=jax.ShapeDtypeStruct((TOK, HEADS * HEAD), BF16),
        compiler_params=pltpu.CompilerParams(vmem_limit_bytes=VMEM),
        name="unpack",
    )(row, back)


def token_ranks(row):
    row = row.astype(F32)
    above, across = iota((TOK, TOK), 0), iota((TOK, TOK), 1)
    col = jnp.sum(jnp.where(above == across, row, 0.0), axis=1, keepdims=True)
    same = col == row
    second = jnp.sum((same & (above < across)).astype(F32), axis=0, keepdims=True)
    second_col = jnp.sum((same & (across < above)).astype(F32), axis=1, keepdims=True)
    group, group_col = jnp.floor(row / POOL), jnp.floor(col / POOL)
    lower = (second_col > 0.5) & (group_col == group) & (col < row)
    rank = jnp.sum(lower.astype(F32), axis=0, keepdims=True)
    return row, group, second, rank


def bits(mask):
    return mask.astype(F32).astype(BF16)


def lean_pack_kernel(
    row_ref, q_ref, k_ref, v_ref, out_ref, first_scr, empty_scr, notes_scr, chosen_scr
):
    @pl.when(pl.program_id(0) == 0)
    def prepare():
        row, group, second, rank = token_ranks(row_ref[...])
        is_second = second > 0.5
        mine = iota((CLUSTERS, TOK), 0).astype(F32) == row
        first = mine & jnp.logical_not(is_second)
        first_scr[...] = bits(first)
        filled = jnp.sum(first.astype(F32), axis=1, keepdims=True) > 0.5
        empty_scr[...] = jnp.where(filled | (iota((1, HEAD), 1) > 0), 0.0, EMPTY)

        seconds = (mine & is_second).astype(F32)
        there = jnp.sum(seconds, axis=1, keepdims=True) > 0.5
        code = jnp.where(there, jnp.sum(seconds * rank, axis=1, keepdims=True), NONE)
        short = jnp.max(second * (rank + 1.0), axis=1, keepdims=True) > EXTRA + 0.5
        place, lane = iota((CLUSTERS, HEAD), 0) % POOL, iota((CLUSTERS, HEAD), 1)
        codes = jnp.where(lane == place, code, 0.0)
        codes = jnp.where((lane == POOL) & short, 1.0, codes).astype(BF16)
        size = CLUSTERS // POOL * TAIL
        number = iota((size, CLUSTERS), 0)
        last = (number % TAIL == TAIL - 1) & (number // TAIL == iota((size, CLUSTERS), 1) // POOL)
        notes_scr[...] = dot(bits(last), codes)

        fits = is_second & (rank < EXTRA - 0.5)
        slot = jnp.where(fits, group * TAIL + rank, -1000.0)
        number = number.astype(F32)
        chosen_scr[...] = jnp.concatenate(
            [bits(number == slot + EXTRA * i) for i in range(3)], axis=1
        )

    data = [ref[...] for ref in (q_ref, k_ref, v_ref)]
    tail = dot(chosen_scr[...], jnp.concatenate(data, axis=0))
    tail = tail + jnp.concatenate([notes_scr[...]] * WIDE, axis=1)
    q, k, v = [dot(first_scr[...], one) for one in data]
    k = k + jnp.concatenate([empty_scr[...]] * WIDE, axis=1)
    for j in range(CLUSTERS // SHARE):
        rows = slice(j * SHARE, (j + 1) * SHARE)
        message = jnp.concatenate(
            [q[rows], k[rows], v[rows], tail[j * HALF : (j + 1) * HALF]], axis=0
        ).astype(BF16)
        for h in range(WIDE):
            place = (j // PAIR, h // CHIPS, j % PAIR, h % CHIPS)
            out_ref[place] = message[:, h * HEAD : (h + 1) * HEAD]


def lean_pack(row, queries, keys, values):
    data = pl.BlockSpec((TOK, WIDE * HEAD), lambda g: (0, g))
    shape = (CLUSTERS // POOL, HEADS // CHIPS, PAIR, CHIPS, MESSAGE, HEAD)
    block = shape[:1] + (WIDE // CHIPS,) + shape[2:]
    tails = CLUSTERS // POOL * TAIL
    return pl.pallas_call(
        lean_pack_kernel,
        grid=(HEADS // WIDE,),
        in_specs=[pl.BlockSpec((1, TOK), lambda g: (0, 0)), data, data, data],
        out_specs=pl.BlockSpec(block, lambda g: (0, g, 0, 0, 0, 0)),
        out_shape=jax.ShapeDtypeStruct(shape, BF16),
        scratch_shapes=[
            pltpu.VMEM((CLUSTERS, TOK), BF16),
            pltpu.VMEM((CLUSTERS, HEAD), F32),
            pltpu.VMEM((tails, HEAD), F32),
            pltpu.VMEM((tails, 3 * TOK), BF16),
        ],
        compiler_params=pltpu.CompilerParams(vmem_limit_bytes=VMEM),
        name="lean_pack",
    )(row, queries, keys, values)


def lean_attend_kernel(
    side_ref, in_ref, other_ref, out_ref, flag_ref, k_scr, v_scr, q_scr, o_scr, code_scr
):
    step = pl.program_id(0)
    side = side_ref[0]
    size = SHARE * CHUNK
    row, col = iota((size, size), 0), iota((size, size), 1)
    turn = bits(col == row % CHUNK * SHARE + row // CHUNK)
    turn_back = bits(row == col % CHUNK * SHARE + col // CHUNK)
    lane = iota((size, HEAD), 1)
    own_lane = lane == iota((size, HEAD), 0) // CHUNK + side * SHARE
    wide_row, wide_col = iota((size, CHUNK * TAIL), 0), iota((size, CHUNK * TAIL), 1)
    own_tail = wide_row % CHUNK == wide_col // TAIL
    wide_col = (wide_col + side * HALF) % TAIL
    pick_notes = bits(own_tail & (wide_col == TAIL - 1))
    tail_place = jnp.where(own_tail, wide_col.astype(F32), -200.0)
    back_place = jnp.where(row % CHUNK == col // SHARE, (col % SHARE).astype(F32), -200.0)

    def keep(part, start, q, k, v):
        shape = (SHARE, CHUNK, HEAD)
        q_scr[:, part : part + CHUNK, :] = q.astype(BF16).reshape(shape)
        v_scr[:, start : start + CHUNK, :] = v.astype(BF16).reshape(shape)
        k_scr[:, start : start + CHUNK, :HEAD] = k.astype(BF16).reshape(shape)
        mark = jnp.where(k > EMPTY / 2, MASKED, 0.0)
        k_scr[:, start : start + CHUNK, HEAD:] = mark.astype(BF16).reshape(shape)

    def load_all(here):
        flags = jnp.zeros((size, HEAD), F32)
        for block in range(SOURCES // CHUNK):
            part = in_ref[block * CHUNK : (block + 1) * CHUNK, :, :].astype(F32)
            pieces = [part[:, i * SHARE : (i + 1) * SHARE].reshape(size, HEAD) for i in range(3)]
            tall = jnp.concatenate(pieces, axis=1)
            mixed = dot(turn, tall.astype(BF16))
            start = here + block * CHUNK
            keep(block * CHUNK, start, mixed[:, :HEAD], mixed[:, HEAD : 2 * HEAD], mixed[:, 2 * HEAD :])

            other = other_ref[block * CHUNK : (block + 1) * CHUNK, :, :].astype(F32)
            tail = jnp.concatenate([part[:, 3 * SHARE :], other], axis=1)
            tail = tail.reshape(CHUNK * TAIL, HEAD).astype(BF16)
            notes = dot(pick_notes, tail)
            flags = jnp.maximum(flags, notes)
            code = jnp.sum(jnp.where(own_lane, notes, 0.0), axis=1, keepdims=True)
            code_scr[block] = jnp.broadcast_to(code, (size, HEAD))
            chosen = jnp.concatenate([bits(tail_place == code + EXTRA * i) for i in range(3)], axis=0)
            found = dot(chosen, tail)
            k = found[size : 2 * size] + jnp.where((code < NONE / 2) & (lane == 0), EMPTY, 0.0)
            start = here + SOURCES + block * CHUNK
            keep(SOURCES + block * CHUNK, start, found[:size], k, found[2 * size :])

        flags = jnp.max(flags, axis=0, keepdims=True)
        if here:
            flags = jnp.maximum(flags, flag_ref[0:1, :])
        flag_ref[...] = jnp.broadcast_to(flags, flag_ref.shape)

    def queries_of(block):
        start, stop = block * QBLK, (block + 1) * QBLK
        unit = bits(iota((QBLK, HEAD), 1) == 0)
        row, col = iota((QBLK, 1), 0), iota((1, QBLK), 1)
        row, col = [one % SOURCES * MOST + one // SOURCES for one in (row, col)]
        later = col > row
        ones = jnp.ones((stop, HEAD), BF16)
        for c in range(SHARE):
            q = jnp.concatenate([q_scr[c], unit], axis=1)
            v = jnp.concatenate([v_scr[c, 0:stop, :], ones], axis=1)
            scores = lax.dot_general(
                q, k_scr[c, 0:stop, :], (((1,), (1,)), ((), ())), preferred_element_type=F32
            )
            last = jnp.where(later, MASKED, scores[:, start:stop])
            if block:
                scores = jnp.concatenate([scores[:, :start], last], axis=1)
            else:
                scores = last
            top = jnp.max(scores, axis=1, keepdims=True)
            weights = jnp.exp2((scores - top) * FACTOR)
            mixed = dot(weights.astype(BF16), v)
            o_scr[c] = (mixed[:, :HEAD] / mixed[:, HEAD:]).astype(BF16)

    def store_all():
        for block in range(SOURCES // CHUNK):
            begin = block * CHUNK
            shape = (CHUNK, SHARE, HEAD)
            firsts = dot(turn_back, o_scr[:, begin : begin + CHUNK, :].reshape(size, HEAD))
            begin = begin + SOURCES
            chosen = bits(back_place == code_scr[block])
            seconds = lax.dot_general(
                chosen,
                o_scr[:, begin : begin + CHUNK, :].reshape(size, HEAD),
                (((0,), (0,)), ((), ())),
                preferred_element_type=F32,
            )
            both = jnp.concatenate([firsts.reshape(shape), seconds.reshape(shape)], axis=1)
            out_ref[block * CHUNK : (block + 1) * CHUNK, :, :] = both.astype(BF16)

    def work(number):
        load_all(number * QBLK)
        queries_of(number)
        store_all()

    for block in range(ROWS // QBLK):
        pl.when(step == block)(lambda block=block: work(block))


def lean_attend(side, received, other):
    part = pltpu.VMEM((SHARE, QBLK, HEAD), BF16)
    return pl.pallas_call(
        lean_attend_kernel,
        grid=(ROWS // QBLK,),
        in_specs=[
            pl.BlockSpec(memory_space=pltpu.SMEM),
            pl.BlockSpec((SOURCES, MESSAGE, HEAD), lambda b: (b, 0, 0)),
            pl.BlockSpec((SOURCES, HALF, HEAD), lambda b: (b, 0, 0)),
        ],
        out_specs=[
            pl.BlockSpec((SOURCES, UNIT, HEAD), lambda b: (b, 0, 0)),
            pl.BlockSpec((8, HEAD), lambda b: (0, 0)),
        ],
        out_shape=[
            jax.ShapeDtypeStruct((DEVICES, UNIT, HEAD), BF16),
            jax.ShapeDtypeStruct((8, HEAD), F32),
        ],
        scratch_shapes=[
            pltpu.VMEM((SHARE, ROWS, 2 * HEAD), BF16),
            pltpu.VMEM((SHARE, ROWS, HEAD), BF16),
            part,
            part,
            pltpu.VMEM((SOURCES // CHUNK, SHARE * CHUNK, HEAD), F32),
        ],
        compiler_params=pltpu.CompilerParams(vmem_limit_bytes=ALL_VMEM),
        name="lean_attend",
    )(side, received, other)


def tail_kernel(in_ref, out_ref):
    out_ref[...] = in_ref[...].astype(F32)[:, HALF:, :].astype(BF16)


def tails_of(received):
    return pl.pallas_call(
        tail_kernel,
        grid=(PAIR,),
        in_specs=[pl.BlockSpec((DEVICES // PAIR, TAIL, HEAD), lambda b: (b, 1, 0))],
        out_specs=pl.BlockSpec((DEVICES // PAIR, HALF, HEAD), lambda b: (b, 0, 0)),
        out_shape=jax.ShapeDtypeStruct((DEVICES, HALF, HEAD), BF16),
        compiler_params=pltpu.CompilerParams(vmem_limit_bytes=ALL_VMEM),
        name="tails",
    )(received)


def lean_unpack_kernel(row_ref, in_ref, out_ref, onehot_scr):
    @pl.when(pl.program_id(0) == 0)
    def prepare():
        row, _, second, rank = token_ranks(row_ref[...])
        owner = jnp.floor(row / SHARE)
        slot = owner * UNIT + jnp.where(second > 0.5, SHARE + rank, row - owner * SHARE)
        onehot_scr[...] = bits(iota(onehot_scr.shape, 0).astype(F32) == slot)

    rows = jnp.concatenate(
        [
            jnp.concatenate(
                [in_ref[j // PAIR, h // CHIPS, j % PAIR, h % CHIPS] for h in range(WIDE)], axis=1
            )
            for j in range(CLUSTERS // SHARE)
        ],
        axis=0,
    )
    out_ref[...] = lax.dot_general(
        onehot_scr[...], rows, (((0,), (0,)), ((), ())), preferred_element_type=F32
    ).astype(BF16)


def lean_unpack(row, back):
    block = (CLUSTERS // POOL, WIDE // CHIPS, PAIR, CHIPS, UNIT, HEAD)
    return pl.pallas_call(
        lean_unpack_kernel,
        grid=(HEADS // WIDE,),
        in_specs=[
            pl.BlockSpec((1, TOK), lambda g: (0, 0)),
            pl.BlockSpec(block, lambda g: (0, g, 0, 0, 0, 0)),
        ],
        out_specs=pl.BlockSpec((TOK, WIDE * HEAD), lambda g: (0, g)),
        out_shape=jax.ShapeDtypeStruct((TOK, HEADS * HEAD), BF16),
        scratch_shapes=[pltpu.VMEM((CLUSTERS // SHARE * UNIT, TOK), BF16)],
        compiler_params=pltpu.CompilerParams(vmem_limit_bytes=ALL_VMEM),
        name="lean_unpack",
    )(row, back)


def exchange(data):
    return lax.all_to_all(data, ("seq", "blk"), split_axis=0, concat_axis=0, tiled=True)


def body(queries, keys, values, cluster_ids):
    row = cluster_ids.reshape(1, TOK)
    sent = lean_pack(row, queries, keys, values)
    received = exchange(sent.reshape(DEVICES, MESSAGE, HEAD))
    swap = [(i, i ^ 1) for i in range(CLUSTERS)]
    other = lax.ppermute(tails_of(received), "seq", swap)
    side = (lax.axis_index("seq") % PAIR).astype(jnp.int32).reshape(1)
    mixed, flags = lean_attend(side, received, other)
    back = exchange(mixed)
    short = flags[0, POOL] > 0.5

    def lean(back, row, queries, keys, values):
        back = back.reshape(CLUSTERS // POOL, HEADS // CHIPS, PAIR, CHIPS, UNIT, HEAD)
        return lean_unpack(row, back)

    def full(back, row, queries, keys, values):
        sent = pack(row, queries, keys, values)
        back = exchange(attend(exchange(sent.reshape(DEVICES, 3 * UNIT, HEAD))))
        return unpack(row, back.reshape(CLUSTERS, GROUPS, UNIT, HEAD))

    return lax.cond(short, full, lean, back, row, queries, keys, values)


def solution(mesh):
    spec = P(("seq", "blk"), None)
    return jax.shard_map(
        body, mesh=mesh, in_specs=(spec,) * 4, out_specs=spec, check_vma=False
    )
```

```python
import jax
import jax.numpy as jnp
from jax import lax
from jax.experimental import pallas as pl
from jax.experimental.pallas import tpu as pltpu
from jax.sharding import PartitionSpec as P

HEADS = 32
HEAD = 128
TOK = 128
CLUSTERS = 128
MOST = 2
GROUPS = 4
SHARE = HEADS // GROUPS
UNIT = SHARE * MOST
DEVICES = CLUSTERS * GROUPS
ROWS = DEVICES * MOST
QBLK = 256
SOURCES = QBLK // MOST
CHUNK = 16
VMEM = 56 * 1024 * 1024
ALL_VMEM = 63 * 1024 * 1024
PAIR = 2
POOL = PAIR * SHARE
EXTRA = 5
TAIL = 16
HALF = TAIL // PAIR
MESSAGE = 3 * SHARE + HALF
CHIPS = 4
WIDE = 16
NONE = -64.0
EMPTY = 256.0
MASKED = -1e30
FACTOR = 1.4426950408889634 / HEAD**0.5
BF16 = jnp.bfloat16
F32 = jnp.float32


def iota(shape, dim):
    return lax.broadcasted_iota(jnp.int32, shape, dim)


def spread_matrix(inverse):
    size = CHUNK * UNIT
    out, src = iota((size, size), 0), iota((size, size), 1)
    if inverse:
        out, src = src, out
    h, d, s = out // (CHUNK * MOST), (out // MOST) % CHUNK, out % MOST
    return (src == d * UNIT + h * MOST + s).astype(F32).astype(BF16)


def slot_onehot(row):
    row = row.astype(F32)
    above, across = iota((TOK, TOK), 0), iota((TOK, TOK), 1)
    col = jnp.sum(jnp.where(above == across, row, 0.0), axis=1, keepdims=True)
    earlier = (col == row) & (above < across)
    slots = row * MOST + jnp.sum(earlier.astype(F32), axis=0, keepdims=True)
    return (iota((CLUSTERS * MOST, TOK), 0).astype(F32) == slots).astype(F32)


def dot(a, b):
    return jnp.dot(a, b, preferred_element_type=F32)


def pack_kernel(row_ref, q_ref, k_ref, v_ref, out_ref):
    onehot = slot_onehot(row_ref[...])
    filled = jnp.sum(onehot, axis=1, keepdims=True) > 0.5
    onehot = onehot.astype(BF16)
    empty_entry = jnp.where(filled | (iota((1, HEAD), 1) > 0), 0.0, EMPTY)
    empty_entry = jnp.concatenate([empty_entry] * SHARE, axis=1)
    scatter = spread_matrix(True)
    rows = [dot(onehot, ref[...]) for ref in (q_ref, k_ref, v_ref)]
    rows[1] = rows[1] + empty_entry
    rows = [one.astype(BF16) for one in rows]
    width = CHUNK * MOST
    for block in range(CLUSTERS // CHUNK):
        tall = jnp.concatenate(
            [
                jnp.concatenate(
                    [
                        one[block * width : (block + 1) * width, h * HEAD : (h + 1) * HEAD]
                        for h in range(SHARE)
                    ],
                    axis=0,
                )
                for one in rows
            ],
            axis=1,
        )
        mixed = dot(scatter, tall).astype(BF16)
        for index in range(3):
            out_ref[
                block * CHUNK : (block + 1) * CHUNK, 0, index * UNIT : (index + 1) * UNIT, :
            ] = mixed[:, index * HEAD : (index + 1) * HEAD].reshape(CHUNK, UNIT, HEAD)


def pack(row, queries, keys, values):
    data = pl.BlockSpec((TOK, SHARE * HEAD), lambda g: (0, g))
    return pl.pallas_call(
        pack_kernel,
        grid=(GROUPS,),
        in_specs=[pl.BlockSpec((1, TOK), lambda g: (0, 0)), data, data, data],
        out_specs=pl.BlockSpec((CLUSTERS, 1, 3 * UNIT, HEAD), lambda g: (0, g, 0, 0)),
        out_shape=jax.ShapeDtypeStruct((CLUSTERS, GROUPS, 3 * UNIT, HEAD), BF16),
        compiler_params=pltpu.CompilerParams(vmem_limit_bytes=VMEM),
        name="pack",
    )(row, queries, keys, values)


def attend_kernel(in_ref, out_ref, k_scr, v_scr, q_scr, o_scr, mark_scr):
    step = pl.program_id(0)
    gather, scatter = spread_matrix(False), spread_matrix(True)
    first_lane = iota((QBLK, HEAD), 1) == 0

    def regroup(block):
        part = in_ref[block * CHUNK : (block + 1) * CHUNK, :, :]
        tall = jnp.concatenate(
            [
                part[:, i * UNIT : (i + 1) * UNIT, :].reshape(CHUNK * UNIT, HEAD)
                for i in range(3)
            ],
            axis=1,
        )
        mixed = dot(gather, tall).astype(BF16)
        width = CHUNK * MOST
        start = pl.multiple_of(step * QBLK + block * width, width)
        q_scr[:, block * width : (block + 1) * width, :] = mixed[:, :HEAD].reshape(
            SHARE, width, HEAD
        )
        k_scr[:, pl.ds(start, width), :] = mixed[:, HEAD : 2 * HEAD].reshape(SHARE, width, HEAD)
        v_scr[:, pl.ds(start, width), :] = mixed[:, 2 * HEAD :].reshape(SHARE, width, HEAD)

    for block in range(SOURCES // CHUNK):
        regroup(block)

    here = pl.multiple_of(step * QBLK, QBLK)
    empty = k_scr[0, pl.ds(here, QBLK), :].astype(F32) > EMPTY / 2
    mark_scr[pl.ds(here, QBLK), :] = jnp.where(empty & first_lane, MASKED, 0.0).astype(BF16)

    def queries_of(block):
        start, stop = block * QBLK, (block + 1) * QBLK
        unit = first_lane.astype(F32).astype(BF16)
        later = iota((QBLK, QBLK), 1) > iota((QBLK, QBLK), 0)
        ones = jnp.ones((stop, HEAD), BF16)
        for h in range(SHARE):
            q = jnp.concatenate([q_scr[h], unit], axis=1)
            k = jnp.concatenate([k_scr[h, 0:stop, :], mark_scr[0:stop, :]], axis=1)
            v = jnp.concatenate([v_scr[h, 0:stop, :], ones], axis=1)
            scores = lax.dot_general(
                q, k, (((1,), (1,)), ((), ())), preferred_element_type=F32
            )
            last = jnp.where(later, MASKED, scores[:, start:stop])
            if block:
                scores = jnp.concatenate([scores[:, :start], last], axis=1)
            else:
                scores = last
            top = jnp.max(scores, axis=1, keepdims=True)
            weights = jnp.exp2((scores - top) * FACTOR)
            mixed = dot(weights.astype(BF16), v)
            o_scr[h] = (mixed[:, :HEAD] / mixed[:, HEAD:]).astype(BF16)

    for block in range(ROWS // QBLK):
        pl.when(step == block)(lambda block=block: queries_of(block))

    for block in range(SOURCES // CHUNK):
        width = CHUNK * MOST
        tall = o_scr[:, block * width : (block + 1) * width, :].reshape(CHUNK * UNIT, HEAD)
        mixed = dot(scatter, tall).astype(BF16)
        out_ref[block * CHUNK : (block + 1) * CHUNK, :, :] = mixed.reshape(CHUNK, UNIT, HEAD)


def attend(received):
    held = pltpu.VMEM((SHARE, ROWS, HEAD), BF16)
    part = pltpu.VMEM((SHARE, QBLK, HEAD), BF16)
    return pl.pallas_call(
        attend_kernel,
        grid=(ROWS // QBLK,),
        in_specs=[pl.BlockSpec((SOURCES, 3 * UNIT, HEAD), lambda b: (b, 0, 0))],
        out_specs=pl.BlockSpec((SOURCES, UNIT, HEAD), lambda b: (b, 0, 0)),
        out_shape=jax.ShapeDtypeStruct((DEVICES, UNIT, HEAD), BF16),
        scratch_shapes=[held, held, part, part, pltpu.VMEM((ROWS, HEAD), BF16)],
        compiler_params=pltpu.CompilerParams(vmem_limit_bytes=VMEM),
        name="attend",
    )(received)


def unpack_kernel(row_ref, in_ref, out_ref):
    onehot = slot_onehot(row_ref[...]).astype(BF16)
    gather = spread_matrix(False)
    width = CHUNK * MOST
    blocks = []
    for block in range(CLUSTERS // CHUNK):
        tall = in_ref[block * CHUNK : (block + 1) * CHUNK, 0, :, :].reshape(CHUNK * UNIT, HEAD)
        mixed = dot(gather, tall).astype(BF16)
        blocks.append(
            jnp.concatenate([mixed[h * width : (h + 1) * width, :] for h in range(SHARE)], axis=1)
        )
    rows = jnp.concatenate(blocks, axis=0)
    out_ref[...] = lax.dot_general(
        onehot, rows, (((0,), (0,)), ((), ())), preferred_element_type=F32
    ).astype(BF16)


def unpack(row, back):
    return pl.pallas_call(
        unpack_kernel,
        grid=(GROUPS,),
        in_specs=[
            pl.BlockSpec((1, TOK), lambda g: (0, 0)),
            pl.BlockSpec((CLUSTERS, 1, UNIT, HEAD), lambda g: (0, g, 0, 0)),
        ],
        out_specs=pl.BlockSpec((TOK, SHARE * HEAD), lambda g: (0, g)),
        out_shape=jax.ShapeDtypeStruct((TOK, HEADS * HEAD), BF16),
        compiler_params=pltpu.CompilerParams(vmem_limit_bytes=VMEM),
        name="unpack",
    )(row, back)


def token_ranks(row):
    row = row.astype(F32)
    above, across = iota((TOK, TOK), 0), iota((TOK, TOK), 1)
    col = jnp.sum(jnp.where(above == across, row, 0.0), axis=1, keepdims=True)
    same = col == row
    second = jnp.sum((same & (above < across)).astype(F32), axis=0, keepdims=True)
    second_col = jnp.sum((same & (across < above)).astype(F32), axis=1, keepdims=True)
    group, group_col = jnp.floor(row / POOL), jnp.floor(col / POOL)
    lower = (second_col > 0.5) & (group_col == group) & (col < row)
    rank = jnp.sum(lower.astype(F32), axis=0, keepdims=True)
    return row, group, second, rank


def bits(mask):
    return mask.astype(F32).astype(BF16)


def lean_pack_kernel(
    row_ref, q_ref, k_ref, v_ref, out_ref, first_scr, empty_scr, notes_scr, chosen_scr
):
    @pl.when(pl.program_id(0) == 0)
    def prepare():
        row, group, second, rank = token_ranks(row_ref[...])
        is_second = second > 0.5
        mine = iota((CLUSTERS, TOK), 0).astype(F32) == row
        first = mine & jnp.logical_not(is_second)
        first_scr[...] = bits(first)
        filled = jnp.sum(first.astype(F32), axis=1, keepdims=True) > 0.5
        empty_scr[...] = jnp.where(filled | (iota((1, HEAD), 1) > 0), 0.0, EMPTY)

        seconds = (mine & is_second).astype(F32)
        there = jnp.sum(seconds, axis=1, keepdims=True) > 0.5
        code = jnp.where(there, jnp.sum(seconds * rank, axis=1, keepdims=True), NONE)
        short = jnp.max(second * (rank + 1.0), axis=1, keepdims=True) > EXTRA + 0.5
        place, lane = iota((CLUSTERS, HEAD), 0) % POOL, iota((CLUSTERS, HEAD), 1)
        codes = jnp.where(lane == place, code, 0.0)
        codes = jnp.where((lane == POOL) & short, 1.0, codes).astype(BF16)
        size = CLUSTERS // POOL * TAIL
        number = iota((size, CLUSTERS), 0)
        last = (number % TAIL == TAIL - 1) & (number // TAIL == iota((size, CLUSTERS), 1) // POOL)
        notes_scr[...] = dot(bits(last), codes)

        fits = is_second & (rank < EXTRA - 0.5)
        slot = jnp.where(fits, group * TAIL + rank, -1000.0)
        number = number.astype(F32)
        chosen_scr[...] = jnp.concatenate(
            [bits(number == slot + EXTRA * i) for i in range(3)], axis=1
        )

    data = [ref[...] for ref in (q_ref, k_ref, v_ref)]
    tail = dot(chosen_scr[...], jnp.concatenate(data, axis=0))
    tail = tail + jnp.concatenate([notes_scr[...]] * WIDE, axis=1)
    q, k, v = [dot(first_scr[...], one) for one in data]
    k = k + jnp.concatenate([empty_scr[...]] * WIDE, axis=1)
    for j in range(CLUSTERS // SHARE):
        rows = slice(j * SHARE, (j + 1) * SHARE)
        message = jnp.concatenate(
            [q[rows], k[rows], v[rows], tail[j * HALF : (j + 1) * HALF]], axis=0
        ).astype(BF16)
        for h in range(WIDE):
            place = (j // PAIR, h // CHIPS, j % PAIR, h % CHIPS)
            out_ref[place] = message[:, h * HEAD : (h + 1) * HEAD]


def lean_pack(row, queries, keys, values):
    data = pl.BlockSpec((TOK, WIDE * HEAD), lambda g: (0, g))
    shape = (CLUSTERS // POOL, HEADS // CHIPS, PAIR, CHIPS, MESSAGE, HEAD)
    block = shape[:1] + (WIDE // CHIPS,) + shape[2:]
    tails = CLUSTERS // POOL * TAIL
    return pl.pallas_call(
        lean_pack_kernel,
        grid=(HEADS // WIDE,),
        in_specs=[pl.BlockSpec((1, TOK), lambda g: (0, 0)), data, data, data],
        out_specs=pl.BlockSpec(block, lambda g: (0, g, 0, 0, 0, 0)),
        out_shape=jax.ShapeDtypeStruct(shape, BF16),
        scratch_shapes=[
            pltpu.VMEM((CLUSTERS, TOK), BF16),
            pltpu.VMEM((CLUSTERS, HEAD), F32),
            pltpu.VMEM((tails, HEAD), F32),
            pltpu.VMEM((tails, 3 * TOK), BF16),
        ],
        compiler_params=pltpu.CompilerParams(vmem_limit_bytes=VMEM),
        name="lean_pack",
    )(row, queries, keys, values)


def lean_attend_kernel(
    side_ref, in_ref, other_ref, out_ref, flag_ref, k_scr, v_scr, q_scr, o_scr, code_scr
):
    step = pl.program_id(0)
    side = side_ref[0]
    size = SHARE * CHUNK
    row, col = iota((size, size), 0), iota((size, size), 1)
    turn = bits(col == row % CHUNK * SHARE + row // CHUNK)
    turn_back = bits(row == col % CHUNK * SHARE + col // CHUNK)
    lane = iota((size, HEAD), 1)
    own_lane = lane == iota((size, HEAD), 0) // CHUNK + side * SHARE
    wide_row, wide_col = iota((size, CHUNK * TAIL), 0), iota((size, CHUNK * TAIL), 1)
    own_tail = wide_row % CHUNK == wide_col // TAIL
    wide_col = (wide_col + side * HALF) % TAIL
    pick_notes = bits(own_tail & (wide_col == TAIL - 1))
    tail_place = jnp.where(own_tail, wide_col.astype(F32), -200.0)
    back_place = jnp.where(row % CHUNK == col // SHARE, (col % SHARE).astype(F32), -200.0)

    def keep(part, start, q, k, v):
        shape = (SHARE, CHUNK, HEAD)
        q_scr[:, part : part + CHUNK, :] = q.astype(BF16).reshape(shape)
        v_scr[:, start : start + CHUNK, :] = v.astype(BF16).reshape(shape)
        k_scr[:, start : start + CHUNK, :HEAD] = k.astype(BF16).reshape(shape)
        mark = jnp.where(k > EMPTY / 2, MASKED, 0.0)
        k_scr[:, start : start + CHUNK, HEAD:] = mark.astype(BF16).reshape(shape)

    def load_all(here):
        flags = jnp.zeros((size, HEAD), F32)
        for block in range(SOURCES // CHUNK):
            part = in_ref[block * CHUNK : (block + 1) * CHUNK, :, :].astype(F32)
            pieces = [part[:, i * SHARE : (i + 1) * SHARE].reshape(size, HEAD) for i in range(3)]
            tall = jnp.concatenate(pieces, axis=1)
            mixed = dot(turn, tall.astype(BF16))
            start = here + block * CHUNK
            keep(block * CHUNK, start, mixed[:, :HEAD], mixed[:, HEAD : 2 * HEAD], mixed[:, 2 * HEAD :])

            other = other_ref[block * CHUNK : (block + 1) * CHUNK, :, :].astype(F32)
            tail = jnp.concatenate([part[:, 3 * SHARE :], other], axis=1)
            tail = tail.reshape(CHUNK * TAIL, HEAD).astype(BF16)
            notes = dot(pick_notes, tail)
            flags = jnp.maximum(flags, notes)
            code = jnp.sum(jnp.where(own_lane, notes, 0.0), axis=1, keepdims=True)
            code_scr[block] = jnp.broadcast_to(code, (size, HEAD))
            chosen = jnp.concatenate([bits(tail_place == code + EXTRA * i) for i in range(3)], axis=0)
            found = dot(chosen, tail)
            k = found[size : 2 * size] + jnp.where((code < NONE / 2) & (lane == 0), EMPTY, 0.0)
            start = here + SOURCES + block * CHUNK
            keep(SOURCES + block * CHUNK, start, found[:size], k, found[2 * size :])

        flags = jnp.max(flags, axis=0, keepdims=True)
        if here:
            flags = jnp.maximum(flags, flag_ref[0:1, :])
        flag_ref[...] = jnp.broadcast_to(flags, flag_ref.shape)

    def queries_of(block):
        start, stop = block * QBLK, (block + 1) * QBLK
        unit = bits(iota((QBLK, HEAD), 1) == 0)
        row, col = iota((QBLK, 1), 0), iota((1, QBLK), 1)
        row, col = [one % SOURCES * MOST + one // SOURCES for one in (row, col)]
        later = col > row
        ones = jnp.ones((stop, HEAD), BF16)
        for c in range(SHARE):
            q = jnp.concatenate([q_scr[c], unit], axis=1)
            v = jnp.concatenate([v_scr[c, 0:stop, :], ones], axis=1)
            scores = lax.dot_general(
                q, k_scr[c, 0:stop, :], (((1,), (1,)), ((), ())), preferred_element_type=F32
            )
            last = jnp.where(later, MASKED, scores[:, start:stop])
            if block:
                scores = jnp.concatenate([scores[:, :start], last], axis=1)
            else:
                scores = last
            top = jnp.max(scores, axis=1, keepdims=True)
            weights = jnp.exp2((scores - top) * FACTOR)
            mixed = dot(weights.astype(BF16), v)
            o_scr[c] = (mixed[:, :HEAD] / mixed[:, HEAD:]).astype(BF16)

    def store_all():
        for block in range(SOURCES // CHUNK):
            begin = block * CHUNK
            shape = (CHUNK, SHARE, HEAD)
            firsts = dot(turn_back, o_scr[:, begin : begin + CHUNK, :].reshape(size, HEAD))
            begin = begin + SOURCES
            chosen = bits(back_place == code_scr[block])
            seconds = lax.dot_general(
                chosen,
                o_scr[:, begin : begin + CHUNK, :].reshape(size, HEAD),
                (((0,), (0,)), ((), ())),
                preferred_element_type=F32,
            )
            both = jnp.concatenate([firsts.reshape(shape), seconds.reshape(shape)], axis=1)
            out_ref[block * CHUNK : (block + 1) * CHUNK, :, :] = both.astype(BF16)

    def work(number):
        load_all(number * QBLK)
        queries_of(number)
        store_all()

    for block in range(ROWS // QBLK):
        pl.when(step == block)(lambda block=block: work(block))


def lean_attend(side, received, other):
    part = pltpu.VMEM((SHARE, QBLK, HEAD), BF16)
    return pl.pallas_call(
        lean_attend_kernel,
        grid=(ROWS // QBLK,),
        in_specs=[
            pl.BlockSpec(memory_space=pltpu.SMEM),
            pl.BlockSpec((SOURCES, MESSAGE, HEAD), lambda b: (b, 0, 0)),
            pl.BlockSpec((SOURCES, HALF, HEAD), lambda b: (b, 0, 0)),
        ],
        out_specs=[
            pl.BlockSpec((SOURCES, UNIT, HEAD), lambda b: (b, 0, 0)),
            pl.BlockSpec((8, HEAD), lambda b: (0, 0)),
        ],
        out_shape=[
            jax.ShapeDtypeStruct((DEVICES, UNIT, HEAD), BF16),
            jax.ShapeDtypeStruct((8, HEAD), F32),
        ],
        scratch_shapes=[
            pltpu.VMEM((SHARE, ROWS, 2 * HEAD), BF16),
            pltpu.VMEM((SHARE, ROWS, HEAD), BF16),
            part,
            part,
            pltpu.VMEM((SOURCES // CHUNK, SHARE * CHUNK, HEAD), F32),
        ],
        compiler_params=pltpu.CompilerParams(vmem_limit_bytes=ALL_VMEM),
        name="lean_attend",
    )(side, received, other)


def tail_kernel(in_ref, out_ref):
    out_ref[...] = in_ref[:, HALF:, :]


def tails_of(received):
    return pl.pallas_call(
        tail_kernel,
        grid=(PAIR,),
        in_specs=[pl.BlockSpec((DEVICES // PAIR, TAIL, HEAD), lambda b: (b, 1, 0))],
        out_specs=pl.BlockSpec((DEVICES // PAIR, HALF, HEAD), lambda b: (b, 0, 0)),
        out_shape=jax.ShapeDtypeStruct((DEVICES, HALF, HEAD), BF16),
        compiler_params=pltpu.CompilerParams(vmem_limit_bytes=ALL_VMEM),
        name="tails",
    )(received)


def lean_unpack_kernel(row_ref, in_ref, out_ref, onehot_scr):
    @pl.when(pl.program_id(0) == 0)
    def prepare():
        row, _, second, rank = token_ranks(row_ref[...])
        owner = jnp.floor(row / SHARE)
        slot = owner * UNIT + jnp.where(second > 0.5, SHARE + rank, row - owner * SHARE)
        onehot_scr[...] = bits(iota(onehot_scr.shape, 0).astype(F32) == slot)

    rows = jnp.concatenate(
        [
            jnp.concatenate(
                [in_ref[j // PAIR, h // CHIPS, j % PAIR, h % CHIPS] for h in range(WIDE)], axis=1
            )
            for j in range(CLUSTERS // SHARE)
        ],
        axis=0,
    )
    out_ref[...] = lax.dot_general(
        onehot_scr[...], rows, (((0,), (0,)), ((), ())), preferred_element_type=F32
    ).astype(BF16)


def lean_unpack(row, back):
    block = (CLUSTERS // POOL, WIDE // CHIPS, PAIR, CHIPS, UNIT, HEAD)
    return pl.pallas_call(
        lean_unpack_kernel,
        grid=(HEADS // WIDE,),
        in_specs=[
            pl.BlockSpec((1, TOK), lambda g: (0, 0)),
            pl.BlockSpec(block, lambda g: (0, g, 0, 0, 0, 0)),
        ],
        out_specs=pl.BlockSpec((TOK, WIDE * HEAD), lambda g: (0, g)),
        out_shape=jax.ShapeDtypeStruct((TOK, HEADS * HEAD), BF16),
        scratch_shapes=[pltpu.VMEM((CLUSTERS // SHARE * UNIT, TOK), BF16)],
        compiler_params=pltpu.CompilerParams(vmem_limit_bytes=ALL_VMEM),
        name="lean_unpack",
    )(row, back)


def exchange(data):
    return lax.all_to_all(data, ("seq", "blk"), split_axis=0, concat_axis=0, tiled=True)


def body(queries, keys, values, cluster_ids):
    row = cluster_ids.reshape(1, TOK)
    sent = lean_pack(row, queries, keys, values)
    received = exchange(sent.reshape(DEVICES, MESSAGE, HEAD))
    swap = [(i, i ^ 1) for i in range(CLUSTERS)]
    other = lax.ppermute(tails_of(received), "seq", swap)
    side = (lax.axis_index("seq") % PAIR).astype(jnp.int32).reshape(1)
    mixed, flags = lean_attend(side, received, other)
    back = exchange(mixed)
    short = flags[0, POOL] > 0.5

    def lean(back, row, queries, keys, values):
        back = back.reshape(CLUSTERS // POOL, HEADS // CHIPS, PAIR, CHIPS, UNIT, HEAD)
        return lean_unpack(row, back)

    def full(back, row, queries, keys, values):
        sent = pack(row, queries, keys, values)
        back = exchange(attend(exchange(sent.reshape(DEVICES, 3 * UNIT, HEAD))))
        return unpack(row, back.reshape(CLUSTERS, GROUPS, UNIT, HEAD))

    return lax.cond(short, full, lean, back, row, queries, keys, values)


def solution(mesh):
    spec = P(("seq", "blk"), None)
    return jax.shard_map(
        body, mesh=mesh, in_specs=(spec,) * 4, out_specs=spec, check_vma=False
    )
```
